32 devices in a mesh: span: 4 (over y, core), seq: 8 (over z, x).
Axes of the slice: x: 2, y: 2, z: 4, core: 2. Of those that a mesh axis runs over, the one named last changes fastest.
Arguments:
- qkv: bfloat16 [3, 4, 512, 2048], P(None, 'span', 'seq'), may hold values from -6 to 6
- lengths: int32 [4], replicated, may hold values from 256 to 512, as said below
Outputs:
- attended: bfloat16 [4, 512, 2048], P('span', 'seq')
The draws below stay inside these ranges and needn't reach their ends.
Inputs may be any that keep to these rules, and one draw needn't show every extreme that they name: `lengths`: the live tokens of a span are its first ones; some span is full.
All inputs are finite; a program needn't handle non-finite values.
Results may differ from the reference program's by a relative error of at most 0.0065.
Values may be sent and summed in bfloat16 or wider, within the bound.
A program may use at most 64 MiB of HBM per device.

```python
import jax
import jax.numpy as jnp
from jax import lax

HEADS = 16
HD = 128
TOKC = 512
SPANS = 4


def draw_qkv(key, part):
    feature_count = HEADS * HD
    shape = (3, SPANS, TOKC, feature_count)
    fields = jnp.clip(jax.random.normal(jax.random.fold_in(key, 12), shape, jnp.float32), -6.0, 6.0)
    return fields.astype(jnp.bfloat16)


def draw_lengths(key, part):
    drawn = jax.random.randint(jax.random.fold_in(key, 5), (SPANS,), TOKC // 2, TOKC + 1)
    full_span = jax.random.randint(jax.random.fold_in(key, 6), (), 0, SPANS)
    return jnp.where(jnp.arange(SPANS) == full_span, TOKC, drawn).astype(jnp.int32)


def setup_inputs(seed: int = 0) -> dict:
    keys = jax.random.split(jax.random.key(seed), 3)
    qkv = draw_qkv(jax.random.fold_in(keys[2], 71), 0)
    lengths = draw_lengths(jax.random.fold_in(keys[2], 71), 0)
    return {"qkv": qkv, "lengths": lengths}


masked_fill = -1e30


def block_terms(queries, key_rows, values, key_live):
    scores = jnp.einsum("hqe,hke->hqk", queries.astype(jnp.float32), key_rows.astype(jnp.float32)) * (key_rows.shape[-1] ** -0.5)
    scores = jnp.where(key_live[None, None, :], scores, masked_fill)
    row_peak = jnp.max(scores, axis=-1)
    weights = jnp.where(key_live[None, None, :], jnp.exp(scores - row_peak[..., None]), 0.0).astype(jnp.bfloat16)
    numerator = jnp.einsum("hqk,hke->hqe", weights.astype(jnp.float32), values.astype(jnp.float32))
    weight_sum = jnp.sum(weights.astype(jnp.float32), axis=-1)
    return row_peak, numerator, weight_sum


def combine(first_terms, second_terms):
    row_peak = jnp.maximum(first_terms[0], second_terms[0])
    scale_first = jnp.exp(first_terms[0] - row_peak)
    scale_second = jnp.exp(second_terms[0] - row_peak)
    numerator = first_terms[1] * scale_first[..., None] + second_terms[1] * scale_second[..., None]
    weight_sum = first_terms[2] * scale_first + second_terms[2] * scale_second
    return row_peak, numerator, weight_sum


def reference(qkv, lengths):
    positions = jnp.arange(TOKC)

    def split_heads(rows):
        return rows.reshape(TOKC, HEADS, HD).transpose(1, 0, 2)

    def per_span(span_index):
        queries = split_heads(qkv[0, span_index])
        initial = (jnp.full((HEADS, TOKC), masked_fill, jnp.float32), jnp.zeros((HEADS, TOKC, HD), jnp.float32), jnp.zeros((HEADS, TOKC), jnp.float32))

        def add_block(running, other_index):
            key_rows = split_heads(qkv[1, other_index])
            values = split_heads(qkv[2, other_index])
            key_live = (other_index <= span_index) & (positions < lengths[other_index])
            return combine(running, block_terms(queries, key_rows, values, key_live)), None

        final_terms, unused = lax.scan(add_block, initial, jnp.arange(SPANS))
        attended = final_terms[1] / final_terms[2][..., None]
        attended = attended.transpose(1, 0, 2).reshape(TOKC, HEADS * HD)
        return jnp.where((positions < lengths[span_index])[:, None], attended, 0.0).astype(jnp.bfloat16)

    return lax.map(per_span, jnp.arange(SPANS))
```

```python
import functools

import jax
import jax.numpy as jnp
from jax import lax
from jax.experimental import pallas as pl
from jax.experimental.pallas import tpu as pltpu
from jax.sharding import PartitionSpec as P

HD = 128
MASKED = -1e30
LOG2E = 1.4426950408889634
MESH = pl.DeviceIdType.MESH


def kernel(
    spans, ranks, heads, rows, lengths_ref, qkv_ref, out_ref,
    keys, queries, results,
    pair_send, query_send, result_send, forward_send,
    pair_recv, query_recv, result_recv,
):
    span = lax.axis_index("span")
    me = lax.axis_index("seq")
    tokens = rows * ranks
    query_tile = min(256, tokens)

    barrier = pltpu.get_barrier_semaphore()

    def greet(k, carry):
        pl.semaphore_signal(
            barrier, inc=1, device_id=(span, lax.rem(me + k, ranks)), device_id_type=MESH
        )
        return carry

    lax.fori_loop(1, ranks, greet, 0)

    @pl.when(span > 0)
    def _():
        pl.semaphore_signal(barrier, inc=1, device_id=(span - 1, me), device_id_type=MESH)

    @pl.when(span < spans - 1)
    def _():
        pl.semaphore_signal(barrier, inc=1, device_id=(span + 1, me), device_id_type=MESH)

    def block_rows(rank):
        return pl.ds(pl.multiple_of(rank * rows, rows), rows)

    def columns(rank, h):
        return pl.ds(pl.multiple_of((rank * heads + h) * HD, HD), HD)

    def pair_slot(h, rank, j):
        return keys.at[h, :, j, block_rows(rank), :]

    def query_slot(h, rank):
        return queries.at[h, block_rows(rank), :]

    def offset(i):
        half = (i + 1) // 2
        return ranks // 2 + half - 2 * half * lax.rem(i, 2)

    def pair_source(rank, h):
        return qkv_ref.at[pl.ds(1, 2), 0, :, columns(rank, h)]

    def query_source(rank, h):
        return qkv_ref.at[0, 0, :, columns(rank, h)]

    def own_pair(h):
        return pltpu.make_async_copy(
            pair_source(me, h), pair_slot(h, me, span), pair_recv.at[h, me, span]
        )

    def own_query(h):
        return pltpu.make_async_copy(
            query_source(me, h), query_slot(h, me), query_recv.at[h, me]
        )

    def send_pair(h, rank):
        return pltpu.make_async_remote_copy(
            src_ref=pair_source(rank, h),
            dst_ref=pair_slot(h, me, span),
            send_sem=pair_send.at[h, rank],
            recv_sem=pair_recv.at[h, me, span],
            device_id=(span, rank),
            device_id_type=MESH,
        )

    def send_query(h, rank):
        return pltpu.make_async_remote_copy(
            src_ref=query_source(rank, h),
            dst_ref=query_slot(h, me),
            send_sem=query_send.at[h, rank],
            recv_sem=query_recv.at[h, me],
            device_id=(span, rank),
            device_id_type=MESH,
        )

    def send_result(h, rank):
        return pltpu.make_async_remote_copy(
            src_ref=results.at[h, block_rows(rank), :],
            dst_ref=out_ref.at[0, :, columns(me, h)],
            send_sem=result_send.at[h, rank],
            recv_sem=result_recv.at[h, me],
            device_id=(span, rank),
            device_id_type=MESH,
        )

    def forward(h, rank, j):
        return pltpu.make_async_remote_copy(
            src_ref=pair_slot(h, rank, j),
            dst_ref=pair_slot(h, rank, j),
            send_sem=forward_send.at[h, rank, j],
            recv_sem=pair_recv.at[h, rank, j],
            device_id=(span + 1, me),
            device_id_type=MESH,
        )

    def wait_bytes(ref, sem):
        pltpu.make_async_copy(ref, ref, sem).wait()

    for h in range(heads):
        own_pair(h).start()
        own_query(h).start()

    pl.semaphore_wait(
        barrier,
        ranks - 1 + (span > 0).astype(jnp.int32) + (span < spans - 1).astype(jnp.int32),
    )

    for h in range(heads):

        def start_pair(i, carry, h=h):
            send_pair(h, lax.rem(me + offset(i), ranks)).start()
            return carry

        def start_query(i, carry, h=h):
            send_query(h, lax.rem(me + offset(i), ranks)).start()
            return carry

        lax.fori_loop(0, ranks - 1, start_pair, 0)
        lax.fori_loop(0, ranks - 1, start_query, 0)

    def pass_on(h):
        def one_rank(rank):
            def one_span(i, carry):
                j = span - i
                wait_bytes(pair_slot(h, rank, j), pair_recv.at[h, rank, j])

                @pl.when(span < spans - 1)
                def _():
                    forward(h, rank, j).start()

                return carry

            lax.fori_loop(0, span + 1, one_span, 0)

        one_rank(me)

        def step(i, carry):
            one_rank(lax.rem(me - offset(i) + ranks, ranks))
            return carry

        lax.fori_loop(0, ranks - 1, step, 0)

    def attend(h):
        def wait_query(rank, carry):
            wait_bytes(query_slot(h, rank), query_recv.at[h, rank])
            return carry

        lax.fori_loop(0, ranks, wait_query, 0)
        own_count = lengths_ref[span]

        def one_tile(tile, carry):
            first = pl.multiple_of(tile * query_tile, query_tile)
            q = queries[h, pl.ds(first, query_tile), :]

            def one_span(j, state):
                peak, total, acc = state
                k = keys[h, 0, j]
                v = keys[h, 1, j]
                scores = lax.dot_general(
                    q, k, (((1,), (1,)), ((), ())), preferred_element_type=jnp.float32
                )
                position = lax.broadcasted_iota(jnp.int32, scores.shape, 1)
                scores = jnp.where(position < lengths_ref[j], scores, MASKED)
                new_peak = jnp.maximum(peak, jnp.max(scores, axis=1, keepdims=True))
                weights = jnp.exp2((scores - new_peak) * (LOG2E * HD**-0.5)).astype(jnp.bfloat16)
                scale = jnp.exp2((peak - new_peak) * (LOG2E * HD**-0.5))
                total = total * scale + jnp.sum(
                    weights.astype(jnp.float32), axis=1, keepdims=True
                )
                acc = acc * scale + jnp.dot(weights, v, preferred_element_type=jnp.float32)
                return new_peak, total, acc

            peak, total, acc = lax.fori_loop(
                0,
                span + 1,
                one_span,
                (
                    jnp.full((query_tile, 1), MASKED, jnp.float32),
                    jnp.zeros((query_tile, 1), jnp.float32),
                    jnp.zeros((query_tile, HD), jnp.float32),
                ),
            )
            position = first + lax.broadcasted_iota(jnp.int32, acc.shape, 0)
            value = jnp.where(position < own_count, acc / total, 0.0)
            results[h, pl.ds(first, query_tile), :] = value.astype(jnp.bfloat16)

            def start_result(i, carry):
                rank = tile * (query_tile // rows) + i

                @pl.when(rank != me)
                def _():
                    send_result(h, rank).start()

                @pl.when(rank == me)
                def _():
                    pltpu.make_async_copy(
                        results.at[h, block_rows(me), :],
                        out_ref.at[0, :, columns(me, h)],
                        result_recv.at[h, me],
                    ).start()

                return carry

            lax.fori_loop(0, query_tile // rows, start_result, 0)
            return carry

        lax.fori_loop(0, tokens // query_tile, one_tile, 0)

    for h in range(heads):
        pass_on(h)
        attend(h)

    for h in range(heads):

        def finish(i, carry, h=h):
            rank = lax.rem(me + i, ranks)
            send_pair(h, rank).wait_send()
            send_query(h, rank).wait_send()
            send_result(h, rank).wait_send()
            return carry

        lax.fori_loop(1, ranks, finish, 0)

        @pl.when(span < spans - 1)
        def _(h=h):
            def finish_rank(rank, carry):
                def finish_span(j, carry):
                    forward(h, rank, j).wait_send()
                    return carry

                return lax.fori_loop(0, span + 1, finish_span, carry)

            lax.fori_loop(0, ranks, finish_rank, 0)

        def arrived(rank, carry, h=h):
            wait_bytes(out_ref.at[0, :, columns(rank, h)], result_recv.at[h, rank])
            return carry

        lax.fori_loop(0, ranks, arrived, 0)


def shards(spans, ranks, qkv, lengths):
    rows, features = qkv.shape[2], qkv.shape[3]
    heads = features // HD // ranks
    tokens = rows * ranks
    dma = pltpu.SemaphoreType.DMA
    return pl.pallas_call(
        functools.partial(kernel, spans, ranks, heads, rows),
        out_shape=jax.ShapeDtypeStruct((1, rows, features), jnp.bfloat16),
        in_specs=[
            pl.BlockSpec(memory_space=pltpu.SMEM),
            pl.BlockSpec(memory_space=pl.ANY),
        ],
        out_specs=pl.BlockSpec(memory_space=pl.ANY),
        scratch_shapes=[
            pltpu.VMEM((heads, 2, spans, tokens, HD), jnp.bfloat16),
            pltpu.VMEM((heads, tokens, HD), jnp.bfloat16),
            pltpu.VMEM((heads, tokens, HD), jnp.bfloat16),
            dma((heads, ranks)),
            dma((heads, ranks)),
            dma((heads, ranks)),
            dma((heads, ranks, spans)),
            dma((heads, ranks, spans)),
            dma((heads, ranks)),
            dma((heads, ranks)),
        ],
        compiler_params=pltpu.CompilerParams(
            collective_id=0, has_side_effects=True, vmem_limit_bytes=40 * 2**20
        ),
    )(lengths, qkv)


def solution(mesh):
    in_specs = (P(None, "span", "seq", None), P())
    out_specs = P("span", "seq", None)
    body = functools.partial(shards, mesh.shape["span"], mesh.shape["seq"])
    return jax.shard_map(body, mesh=mesh, in_specs=in_specs, out_specs=out_specs, check_vma=False)
```

```python
import functools

import jax
import jax.numpy as jnp
from jax import lax
from jax.experimental import pallas as pl
from jax.experimental.pallas import tpu as pltpu
from jax.sharding import PartitionSpec as P

HD = 128
MASKED = -1e30
LOG2E = 1.4426950408889634
MESH = pl.DeviceIdType.MESH


def kernel(
    spans, ranks, heads, rows, lengths_hbm, qkv_ref, out_ref,
    keys, queries, results, peaks, totals, sums, lengths_ref, lengths_sem,
    pair_send, query_send, result_send, forward_send,
    pair_recv, query_recv, result_recv,
):
    span = lax.axis_index("span")
    me = lax.axis_index("seq")
    tokens = rows * ranks
    query_tile = min(256, tokens)
    half = ranks // 2

    barrier = pltpu.get_barrier_semaphore()

    def greet(k, carry):
        pl.semaphore_signal(
            barrier, inc=1, device_id=(span, lax.rem(me + k, ranks)), device_id_type=MESH
        )
        return carry

    lax.fori_loop(1, ranks, greet, 0)

    @pl.when(span > 0)
    def _():
        pl.semaphore_signal(barrier, inc=1, device_id=(span - 1, me), device_id_type=MESH)

    @pl.when(span < spans - 1)
    def _():
        pl.semaphore_signal(barrier, inc=1, device_id=(span + 1, me), device_id_type=MESH)

    def block_rows(rank):
        return pl.ds(pl.multiple_of(rank * rows, rows), rows)

    def columns(rank, h):
        return pl.ds(pl.multiple_of((rank * heads + h) * HD, HD), HD)

    def pair_slot(h, rank, j):
        return keys.at[h, :, j, block_rows(rank), :]

    def query_slot(h, rank):
        return queries.at[h, block_rows(rank), :]

    def partner(k):
        total = 0
        for bit in range(ranks.bit_length() - 1):
            unit = 2**bit
            total += lax.rem(me // unit + k // unit, 2) * unit
        return total

    def send_step(i):
        odd = lax.rem(i, 2)
        return odd * ((i + 1) // 2) + (1 - odd) * (half + i // 2)

    def pair_source(rank, h):
        return qkv_ref.at[pl.ds(1, 2), 0, :, columns(rank, h)]

    def query_source(rank, h):
        return qkv_ref.at[0, 0, :, columns(rank, h)]

    def own_pair(h):
        return pltpu.make_async_copy(
            pair_source(me, h), pair_slot(h, me, span), pair_recv.at[h, me, span]
        )

    def own_query(h):
        return pltpu.make_async_copy(
            query_source(me, h), query_slot(h, me), query_recv.at[h, me]
        )

    def send_pair(h, rank):
        return pltpu.make_async_remote_copy(
            src_ref=pair_source(rank, h),
            dst_ref=pair_slot(h, me, span),
            send_sem=pair_send.at[h, rank],
            recv_sem=pair_recv.at[h, me, span],
            device_id=(span, rank),
            device_id_type=MESH,
        )

    def send_query(h, rank):
        return pltpu.make_async_remote_copy(
            src_ref=query_source(rank, h),
            dst_ref=query_slot(h, me),
            send_sem=query_send.at[h, rank],
            recv_sem=query_recv.at[h, me],
            device_id=(span, rank),
            device_id_type=MESH,
        )

    def send_result(h, rank):
        return pltpu.make_async_remote_copy(
            src_ref=results.at[h, block_rows(rank), :],
            dst_ref=out_ref.at[0, :, columns(me, h)],
            send_sem=result_send.at[h, rank],
            recv_sem=result_recv.at[h, me],
            device_id=(span, rank),
            device_id_type=MESH,
        )

    def forward(h, rank, j):
        return pltpu.make_async_remote_copy(
            src_ref=pair_slot(h, rank, j),
            dst_ref=pair_slot(h, rank, j),
            send_sem=forward_send.at[h, rank, j],
            recv_sem=pair_recv.at[h, rank, j],
            device_id=(span + 1, me),
            device_id_type=MESH,
        )

    def wait_bytes(ref, sem):
        pltpu.make_async_copy(ref, ref, sem).wait()

    read_lengths = pltpu.make_async_copy(lengths_hbm, lengths_ref, lengths_sem)
    read_lengths.start()
    for h in range(heads):
        own_pair(h).start()
        own_query(h).start()

    pl.semaphore_wait(
        barrier,
        ranks - 1 + (span > 0).astype(jnp.int32) + (span < spans - 1).astype(jnp.int32),
    )

    for h in range(heads):

        def start_pair(i, carry, h=h):
            send_pair(h, partner(send_step(i))).start()
            return carry

        def start_query(i, carry, h=h):
            send_query(h, partner(send_step(i))).start()
            return carry

        lax.fori_loop(0, ranks - 1, start_pair, 0)
        lax.fori_loop(0, ranks - 1, start_query, 0)

    def pass_on(h, j, first, last):
        def step(k, carry):
            rank = partner(k)
            wait_bytes(pair_slot(h, rank, j), pair_recv.at[h, rank, j])

            @pl.when(span < spans - 1)
            def _():
                forward(h, rank, j).start()

            return carry

        lax.fori_loop(first, last, step, 0)

    def pass_near(h):
        def step(i, carry):
            pass_on(h, span - i, 0, half)
            return carry

        lax.fori_loop(0, span + 1, step, 0)

    def pass_far(h, j):
        pass_on(h, j, half, ranks)

    def wait_queries(h):
        def step(rank, carry):
            wait_bytes(query_slot(h, rank), query_recv.at[h, rank])
            return carry

        lax.fori_loop(0, ranks, step, 0)

    def add_block(h, j, here, live):
        scores = lax.dot_general(
            queries[h, here, :],
            keys[h, 0, j],
            (((1,), (1,)), ((), ())),
            preferred_element_type=jnp.float32,
        )
        position = lax.broadcasted_iota(jnp.int32, scores.shape, 1)
        scores = jnp.where(position < live, scores, MASKED)
        peak = peaks[here, :]
        new_peak = jnp.maximum(peak, jnp.max(scores, axis=1, keepdims=True))
        weights = jnp.exp2((scores - new_peak) * (LOG2E * HD**-0.5)).astype(jnp.bfloat16)
        scale = jnp.exp2((peak - new_peak) * (LOG2E * HD**-0.5))
        total = totals[here, :] * scale + jnp.sum(
            weights.astype(jnp.float32), axis=1, keepdims=True
        )
        acc = sums[here, :] * scale + jnp.dot(
            weights, keys[h, 1, j], preferred_element_type=jnp.float32
        )
        return new_peak, total, acc

    def tile_rows(tile):
        return pl.ds(pl.multiple_of(tile * query_tile, query_tile), query_tile)

    tiles = tokens // query_tile

    def start_state():
        peaks[...] = jnp.full(peaks.shape, MASKED, jnp.float32)
        totals[...] = jnp.zeros(totals.shape, jnp.float32)
        sums[...] = jnp.zeros(sums.shape, jnp.float32)

    def middle_block(h, j):
        def one_tile(tile, carry):
            here = tile_rows(tile)
            peaks[here, :], totals[here, :], sums[here, :] = add_block(
                h, j, here, lengths_ref[j]
            )
            return carry

        lax.fori_loop(0, tiles, one_tile, 0)

    def last_block(h):
        def one_tile(tile, carry):
            here = tile_rows(tile)
            _, total, acc = add_block(h, 0, here, lengths_ref[0])
            position = tile * query_tile + lax.broadcasted_iota(jnp.int32, acc.shape, 0)
            value = jnp.where(position < lengths_ref[span], acc / total, 0.0)
            results[h, here, :] = value.astype(jnp.bfloat16)

            def start_result(i, carry):
                rank = tile * (query_tile // rows) + i

                @pl.when(rank != me)
                def _():
                    send_result(h, rank).start()

                @pl.when(rank == me)
                def _():
                    pltpu.make_async_copy(
                        results.at[h, block_rows(me), :],
                        out_ref.at[0, :, columns(me, h)],
                        result_recv.at[h, me],
                    ).start()

                return carry

            lax.fori_loop(0, query_tile // rows, start_result, 0)
            return carry

        lax.fori_loop(0, tiles, one_tile, 0)

    read_lengths.wait()
    for h in range(heads):
        pass_near(h)
    for h in range(heads):
        start_state()
        pass_far(h, span)

        @pl.when(span > 0)
        def _(h=h):
            pass_far(h, span - 1)

        wait_queries(h)

        def step(i, carry, h=h):
            middle_block(h, span - i)

            @pl.when(i + 1 < span)
            def _():
                pass_far(h, span - i - 2)

            return carry

        lax.fori_loop(0, span, step, 0)
        last_block(h)

    for h in range(heads):

        def finish(i, carry, h=h):
            rank = lax.rem(me + i, ranks)
            send_pair(h, rank).wait_send()
            send_query(h, rank).wait_send()
            send_result(h, rank).wait_send()
            return carry

        lax.fori_loop(1, ranks, finish, 0)

        @pl.when(span < spans - 1)
        def _(h=h):
            def finish_rank(rank, carry):
                def finish_span(j, carry):
                    forward(h, rank, j).wait_send()
                    return carry

                return lax.fori_loop(0, span + 1, finish_span, carry)

            lax.fori_loop(0, ranks, finish_rank, 0)

        def arrived(rank, carry, h=h):
            wait_bytes(out_ref.at[0, :, columns(rank, h)], result_recv.at[h, rank])
            return carry

        lax.fori_loop(0, ranks, arrived, 0)


def shards(spans, ranks, qkv, lengths):
    rows, features = qkv.shape[2], qkv.shape[3]
    heads = features // HD // ranks
    tokens = rows * ranks
    dma = pltpu.SemaphoreType.DMA
    return pl.pallas_call(
        functools.partial(kernel, spans, ranks, heads, rows),
        out_shape=jax.ShapeDtypeStruct((1, rows, features), jnp.bfloat16),
        in_specs=[
            pl.BlockSpec(memory_space=pltpu.HBM),
            pl.BlockSpec(memory_space=pltpu.HBM),
        ],
        out_specs=pl.BlockSpec(memory_space=pl.ANY),
        scratch_shapes=[
            pltpu.VMEM((heads, 2, spans, tokens, HD), jnp.bfloat16),
            pltpu.VMEM((heads, tokens, HD), jnp.bfloat16),
            pltpu.VMEM((heads, tokens, HD), jnp.bfloat16),
            pltpu.VMEM((tokens, 1), jnp.float32),
            pltpu.VMEM((tokens, 1), jnp.float32),
            pltpu.VMEM((tokens, HD), jnp.float32),
            pltpu.SMEM((spans,), jnp.int32),
            dma(()),
            dma((heads, ranks)),
            dma((heads, ranks)),
            dma((heads, ranks)),
            dma((heads, ranks, spans)),
            dma((heads, ranks, spans)),
            dma((heads, ranks)),
            dma((heads, ranks)),
        ],
        compiler_params=pltpu.CompilerParams(
            collective_id=0, has_side_effects=True, vmem_limit_bytes=40 * 2**20
        ),
    )(lengths, qkv)


def solution(mesh):
    in_specs = (P(None, "span", "seq", None), P())
    out_specs = P("span", "seq", None)
    body = functools.partial(shards, mesh.shape["span"], mesh.shape["seq"])
    return jax.shard_map(body, mesh=mesh, in_specs=in_specs, out_specs=out_specs, check_vma=False)
```

```python
import functools

import jax
import jax.numpy as jnp
from jax import lax
from jax.experimental import pallas as pl
from jax.experimental.pallas import tpu as pltpu
from jax.sharding import PartitionSpec as P

HD = 128
MASKED = -1e30
LOG2E = 1.4426950408889634
MESH = pl.DeviceIdType.MESH


def kernel(
    spans, ranks, heads, rows, lengths_hbm, qkv_ref, out_ref,
    keys, queries, results, peaks, totals, sums, lengths_ref, lengths_sem,
    pair_send, query_send, result_send, forward_send,
    pair_recv, query_recv, result_recv,
):
    span = lax.axis_index("span")
    me = lax.axis_index("seq")
    tokens = rows * ranks
    query_tile = min(256, tokens)
    half = ranks // 2

    barrier = pltpu.get_barrier_semaphore()

    def greet(k, carry):
        pl.semaphore_signal(
            barrier, inc=1, device_id=(span, lax.rem(me + k, ranks)), device_id_type=MESH
        )
        return carry

    lax.fori_loop(1, ranks, greet, 0)

    @pl.when(span > 0)
    def _():
        pl.semaphore_signal(barrier, inc=1, device_id=(span - 1, me), device_id_type=MESH)

    @pl.when(span < spans - 1)
    def _():
        pl.semaphore_signal(barrier, inc=1, device_id=(span + 1, me), device_id_type=MESH)

    def block_rows(rank):
        return pl.ds(pl.multiple_of(rank * rows, rows), rows)

    def columns(rank, h):
        return pl.ds(pl.multiple_of((rank * heads + h) * HD, HD), HD)

    def pair_slot(h, rank, j):
        return keys.at[h, :, j, block_rows(rank), :]

    def query_slot(h, rank):
        return queries.at[h, block_rows(rank), :]

    def partner(k):
        total = 0
        for bit in range(ranks.bit_length() - 1):
            unit = 2**bit
            total += lax.rem(me // unit + k // unit, 2) * unit
        return total

    def send_step(i):
        odd = lax.rem(i, 2)
        return odd * ((i + 1) // 2) + (1 - odd) * (half + i // 2)

    def pair_source(rank, h):
        return qkv_ref.at[pl.ds(1, 2), 0, :, columns(rank, h)]

    def query_source(rank, h):
        return qkv_ref.at[0, 0, :, columns(rank, h)]

    def own_pair(h):
        return pltpu.make_async_copy(
            pair_source(me, h), pair_slot(h, me, span), pair_recv.at[h, me, span]
        )

    def own_query(h):
        return pltpu.make_async_copy(
            query_source(me, h), query_slot(h, me), query_recv.at[h, me]
        )

    def send_pair(h, rank):
        return pltpu.make_async_remote_copy(
            src_ref=pair_source(rank, h),
            dst_ref=pair_slot(h, me, span),
            send_sem=pair_send.at[h, rank],
            recv_sem=pair_recv.at[h, me, span],
            device_id=(span, rank),
            device_id_type=MESH,
        )

    def send_query(h, rank):
        return pltpu.make_async_remote_copy(
            src_ref=query_source(rank, h),
            dst_ref=query_slot(h, me),
            send_sem=query_send.at[h, rank],
            recv_sem=query_recv.at[h, me],
            device_id=(span, rank),
            device_id_type=MESH,
        )

    def send_result(h, rank):
        return pltpu.make_async_remote_copy(
            src_ref=results.at[h, block_rows(rank), :],
            dst_ref=out_ref.at[0, :, columns(me, h)],
            send_sem=result_send.at[h, rank],
            recv_sem=result_recv.at[h, me],
            device_id=(span, rank),
            device_id_type=MESH,
        )

    def forward(h, rank, j):
        return pltpu.make_async_remote_copy(
            src_ref=pair_slot(h, rank, j),
            dst_ref=pair_slot(h, rank, j),
            send_sem=forward_send.at[h, rank, j],
            recv_sem=pair_recv.at[h, rank, j],
            device_id=(span + 1, me),
            device_id_type=MESH,
        )

    def wait_bytes(ref, sem):
        pltpu.make_async_copy(ref, ref, sem).wait()

    read_lengths = pltpu.make_async_copy(lengths_hbm, lengths_ref, lengths_sem)
    read_lengths.start()
    for h in range(heads):
        own_pair(h).start()
        own_query(h).start()

    pl.semaphore_wait(
        barrier,
        ranks - 1 + (span > 0).astype(jnp.int32) + (span < spans - 1).astype(jnp.int32),
    )

    groups = [(h, make) for h in range(heads) for make in (send_pair, send_query)]
    in_flight = []

    def start_group(h, make):
        def step(i, carry):
            make(h, partner(send_step(i))).start()
            return carry

        lax.fori_loop(0, ranks - 1, step, 0)

    def drain_group(h, make):
        def step(i, carry):
            make(h, partner(send_step(i))).wait_send()
            return carry

        lax.fori_loop(0, ranks - 1, step, 0)

    def advance():
        if groups:
            if len(in_flight) == 2:
                drain_group(*in_flight.pop(0))
            in_flight.append(groups.pop(0))
            start_group(*in_flight[-1])

    advance()
    advance()

    def pass_on(h, j, first, last):
        def step(k, carry):
            rank = partner(k)
            wait_bytes(pair_slot(h, rank, j), pair_recv.at[h, rank, j])

            @pl.when(span < spans - 1)
            def _():
                forward(h, rank, j).start()

            return carry

        lax.fori_loop(first, last, step, 0)

    def pass_near(h):
        pass_on(h, span, 0, half)
        advance()

        def step(i, carry):
            pass_on(h, span - i, 0, half)
            return carry

        lax.fori_loop(1, span + 1, step, 0)

    def pass_far(h, j):
        pass_on(h, j, half, ranks)

    def wait_queries(h):
        def step(rank, carry):
            wait_bytes(query_slot(h, rank), query_recv.at[h, rank])
            return carry

        lax.fori_loop(0, ranks, step, 0)

    def add_block(h, j, here, live):
        scores = lax.dot_general(
            queries[h, here, :],
            keys[h, 0, j],
            (((1,), (1,)), ((), ())),
            preferred_element_type=jnp.float32,
        )
        position = lax.broadcasted_iota(jnp.int32, scores.shape, 1)
        scores = jnp.where(position < live, scores, MASKED)
        peak = peaks[here, :]
        new_peak = jnp.maximum(peak, jnp.max(scores, axis=1, keepdims=True))
        weights = jnp.exp2((scores - new_peak) * (LOG2E * HD**-0.5)).astype(jnp.bfloat16)
        scale = jnp.exp2((peak - new_peak) * (LOG2E * HD**-0.5))
        total = totals[here, :] * scale + jnp.sum(
            weights.astype(jnp.float32), axis=1, keepdims=True
        )
        acc = sums[here, :] * scale + jnp.dot(
            weights, keys[h, 1, j], preferred_element_type=jnp.float32
        )
        return new_peak, total, acc

    def tile_rows(tile):
        return pl.ds(pl.multiple_of(tile * query_tile, query_tile), query_tile)

    tiles = tokens // query_tile

    def start_state():
        peaks[...] = jnp.full(peaks.shape, MASKED, jnp.float32)
        totals[...] = jnp.zeros(totals.shape, jnp.float32)
        sums[...] = jnp.zeros(sums.shape, jnp.float32)

    def middle_block(h, j):
        def one_tile(tile, carry):
            here = tile_rows(tile)
            peaks[here, :], totals[here, :], sums[here, :] = add_block(
                h, j, here, lengths_ref[j]
            )
            return carry

        lax.fori_loop(0, tiles, one_tile, 0)

    def last_block(h):
        def one_tile(tile, carry):
            here = tile_rows(tile)
            _, total, acc = add_block(h, 0, here, lengths_ref[0])
            position = tile * query_tile + lax.broadcasted_iota(jnp.int32, acc.shape, 0)
            value = jnp.where(position < lengths_ref[span], acc / total, 0.0)
            results[h, here, :] = value.astype(jnp.bfloat16)

            def start_result(i, carry):
                rank = tile * (query_tile // rows) + i

                @pl.when(rank != me)
                def _():
                    send_result(h, rank).start()

                @pl.when(rank == me)
                def _():
                    pltpu.make_async_copy(
                        results.at[h, block_rows(me), :],
                        out_ref.at[0, :, columns(me, h)],
                        result_recv.at[h, me],
                    ).start()

                return carry

            lax.fori_loop(0, query_tile // rows, start_result, 0)
            return carry

        lax.fori_loop(0, tiles, one_tile, 0)

    read_lengths.wait()
    pass_near(0)
    for h in range(heads):
        start_state()
        pass_far(h, span)
        advance()

        @pl.when(span > 0)
        def _(h=h):
            pass_far(h, span - 1)

        wait_queries(h)

        def step(i, carry, h=h):
            middle_block(h, span - i)

            @pl.when(i + 1 < span)
            def _():
                pass_far(h, span - i - 2)

            return carry

        lax.fori_loop(0, span, step, 0)
        if h + 1 < heads:
            pass_near(h + 1)
        last_block(h)

    for group in in_flight:
        drain_group(*group)

    for h in range(heads):

        def finish(i, carry, h=h):
            rank = lax.rem(me + i, ranks)
            send_result(h, rank).wait_send()
            return carry

        lax.fori_loop(1, ranks, finish, 0)

        @pl.when(span < spans - 1)
        def _(h=h):
            def finish_rank(rank, carry):
                def finish_span(j, carry):
                    forward(h, rank, j).wait_send()
                    return carry

                return lax.fori_loop(0, span + 1, finish_span, carry)

            lax.fori_loop(0, ranks, finish_rank, 0)

        def arrived(rank, carry, h=h):
            wait_bytes(out_ref.at[0, :, columns(rank, h)], result_recv.at[h, rank])
            return carry

        lax.fori_loop(0, ranks, arrived, 0)


def shards(spans, ranks, qkv, lengths):
    rows, features = qkv.shape[2], qkv.shape[3]
    heads = features // HD // ranks
    tokens = rows * ranks
    dma = pltpu.SemaphoreType.DMA
    return pl.pallas_call(
        functools.partial(kernel, spans, ranks, heads, rows),
        out_shape=jax.ShapeDtypeStruct((1, rows, features), jnp.bfloat16),
        in_specs=[
            pl.BlockSpec(memory_space=pltpu.HBM),
            pl.BlockSpec(memory_space=pltpu.HBM),
        ],
        out_specs=pl.BlockSpec(memory_space=pl.ANY),
        scratch_shapes=[
            pltpu.VMEM((heads, 2, spans, tokens, HD), jnp.bfloat16),
            pltpu.VMEM((heads, tokens, HD), jnp.bfloat16),
            pltpu.VMEM((heads, tokens, HD), jnp.bfloat16),
            pltpu.VMEM((tokens, 1), jnp.float32),
            pltpu.VMEM((tokens, 1), jnp.float32),
            pltpu.VMEM((tokens, HD), jnp.float32),
            pltpu.SMEM((spans,), jnp.int32),
            dma(()),
            dma((heads, ranks)),
            dma((heads, ranks)),
            dma((heads, ranks)),
            dma((heads, ranks, spans)),
            dma((heads, ranks, spans)),
            dma((heads, ranks)),
            dma((heads, ranks)),
        ],
        compiler_params=pltpu.CompilerParams(
            collective_id=0, has_side_effects=True, vmem_limit_bytes=64 * 2**20
        ),
    )(lengths, qkv)


def solution(mesh):
    in_specs = (P(None, "span", "seq", None), P())
    out_specs = P("span", "seq", None)
    body = functools.partial(shards, mesh.shape["span"], mesh.shape["seq"])
    return jax.shard_map(body, mesh=mesh, in_specs=in_specs, out_specs=out_specs, check_vma=False)
```

```python
import functools

import jax
import jax.numpy as jnp
from jax import lax
from jax.experimental import pallas as pl
from jax.experimental.pallas import tpu as pltpu
from jax.sharding import PartitionSpec as P

HD = 128
MASKED = -1e30
LOG2E = 1.4426950408889634
MESH = pl.DeviceIdType.MESH


def kernel(
    spans, ranks, heads, rows, lengths_hbm, qkv_ref, out_ref,
    keys, queries, results, peaks, sums, lengths_ref, lengths_sem,
    pair_send, query_send, result_send, forward_send,
    pair_recv, query_recv, result_recv,
):
    span = lax.axis_index("span")
    me = lax.axis_index("seq")
    tokens = rows * ranks
    query_tile = min(256, tokens)
    half = ranks // 2

    barrier = pltpu.get_barrier_semaphore()

    def greet(k, carry):
        pl.semaphore_signal(
            barrier, inc=1, device_id=(span, lax.rem(me + k, ranks)), device_id_type=MESH
        )
        return carry

    lax.fori_loop(1, ranks, greet, 0)

    @pl.when(span > 0)
    def _():
        pl.semaphore_signal(barrier, inc=1, device_id=(span - 1, me), device_id_type=MESH)

    @pl.when(span < spans - 1)
    def _():
        pl.semaphore_signal(barrier, inc=1, device_id=(span + 1, me), device_id_type=MESH)

    def block_rows(rank):
        return pl.ds(pl.multiple_of(rank * rows, rows), rows)

    def columns(rank, h):
        return pl.ds(pl.multiple_of((rank * heads + h) * HD, HD), HD)

    def pair_slot(h, rank, j):
        return keys.at[h, :, j, block_rows(rank), :]

    def query_slot(h, rank):
        return queries.at[h, block_rows(rank), :]

    def partner(k):
        total = 0
        for bit in range(ranks.bit_length() - 1):
            unit = 2**bit
            total += lax.rem(me // unit + k // unit, 2) * unit
        return total

    def send_step(i):
        odd = lax.rem(i, 2)
        return odd * ((i + 1) // 2) + (1 - odd) * (half + i // 2)

    def pair_source(rank, h):
        return qkv_ref.at[pl.ds(1, 2), 0, :, columns(rank, h)]

    def query_source(rank, h):
        return qkv_ref.at[0, 0, :, columns(rank, h)]

    def own_pair(h):
        return pltpu.make_async_copy(
            pair_source(me, h), pair_slot(h, me, span), pair_recv.at[h, me, span]
        )

    def own_query(h):
        return pltpu.make_async_copy(
            query_source(me, h), query_slot(h, me), query_recv.at[h, me]
        )

    def send_pair(h, rank):
        return pltpu.make_async_remote_copy(
            src_ref=pair_source(rank, h),
            dst_ref=pair_slot(h, me, span),
            send_sem=pair_send.at[h, rank],
            recv_sem=pair_recv.at[h, me, span],
            device_id=(span, rank),
            device_id_type=MESH,
        )

    def send_query(h, rank):
        return pltpu.make_async_remote_copy(
            src_ref=query_source(rank, h),
            dst_ref=query_slot(h, me),
            send_sem=query_send.at[h, rank],
            recv_sem=query_recv.at[h, me],
            device_id=(span, rank),
            device_id_type=MESH,
        )

    def send_result(h, rank):
        return pltpu.make_async_remote_copy(
            src_ref=results.at[h, block_rows(rank), :],
            dst_ref=out_ref.at[0, :, columns(me, h)],
            send_sem=result_send.at[h, rank],
            recv_sem=result_recv.at[h, me],
            device_id=(span, rank),
            device_id_type=MESH,
        )

    def forward(h, rank, j):
        return pltpu.make_async_remote_copy(
            src_ref=pair_slot(h, rank, j),
            dst_ref=pair_slot(h, rank, j),
            send_sem=forward_send.at[h, rank, j],
            recv_sem=pair_recv.at[h, rank, j],
            device_id=(span + 1, me),
            device_id_type=MESH,
        )

    def wait_bytes(ref, sem):
        pltpu.make_async_copy(ref, ref, sem).wait()

    read_lengths = pltpu.make_async_copy(lengths_hbm, lengths_ref, lengths_sem)
    read_lengths.start()
    for h in range(heads):
        own_pair(h).start()
        own_query(h).start()

    pl.semaphore_wait(
        barrier,
        ranks - 1 + (span > 0).astype(jnp.int32) + (span < spans - 1).astype(jnp.int32),
    )

    groups = [(h, make) for h in range(heads) for make in (send_pair, send_query)]
    in_flight = []

    def start_group(h, make):
        def step(i, carry):
            make(h, partner(send_step(i))).start()
            return carry

        lax.fori_loop(0, ranks - 1, step, 0)

    def drain_group(h, make):
        def step(i, carry):
            make(h, partner(send_step(i))).wait_send()
            return carry

        lax.fori_loop(0, ranks - 1, step, 0)

    def advance():
        if groups:
            if len(in_flight) == 2:
                drain_group(*in_flight.pop(0))
            in_flight.append(groups.pop(0))
            start_group(*in_flight[-1])

    advance()
    advance()

    def pass_on(h, j, first, last):
        def step(k, carry):
            rank = partner(k)
            wait_bytes(pair_slot(h, rank, j), pair_recv.at[h, rank, j])

            @pl.when(span < spans - 1)
            def _():
                forward(h, rank, j).start()

            return carry

        lax.fori_loop(first, last, step, 0)

    def pass_near(h):
        def step(i, carry):
            pass_on(h, span - i, 0, half)
            return carry

        lax.fori_loop(0, span + 1, step, 0)

    def pass_far(h, j):
        pass_on(h, j, half, ranks)

    def wait_queries(h):
        def step(rank, carry):
            wait_bytes(query_slot(h, rank), query_recv.at[h, rank])
            return carry

        lax.fori_loop(0, ranks, step, 0)

    tiles = tokens // query_tile
    side = min(2, tiles)
    ones = jnp.ones((tokens, HD), jnp.bfloat16)

    def add_block(h, j, first):
        live = lax.broadcasted_iota(jnp.int32, (1, tokens), 1) < lengths_ref[j]
        limit = jnp.where(live, -2 * MASKED, MASKED)
        k = keys[h, 0, j]
        v = jnp.concatenate([keys[h, 1, j], ones], axis=1)
        states = []
        for t in range(side):
            here = pl.ds(first + t * query_tile, query_tile)
            scores = lax.dot_general(
                queries[h, here, :],
                k,
                (((1,), (1,)), ((), ())),
                preferred_element_type=jnp.float32,
            )
            scores = jnp.minimum(scores, limit)
            peak = peaks[here, :]
            new_peak = jnp.maximum(peak, jnp.max(scores, axis=1, keepdims=True))
            weights = jnp.exp2((scores - new_peak) * (LOG2E * HD**-0.5)).astype(jnp.bfloat16)
            scale = jnp.exp2((peak - new_peak) * (LOG2E * HD**-0.5))
            acc = sums[here, :] * scale + jnp.dot(
                weights, v, preferred_element_type=jnp.float32
            )
            states.append((here, new_peak, acc))
        return states

    def start_state():
        peaks[...] = jnp.full(peaks.shape, MASKED, jnp.float32)
        sums[...] = jnp.zeros(sums.shape, jnp.float32)

    def each_group(body):
        if tiles == side:
            body(0)
        else:

            def step(group, carry):
                body(pl.multiple_of(group * side * query_tile, side * query_tile))
                return carry

            lax.fori_loop(0, tiles // side, step, 0)

    def middle_block(h, j):
        def body(first):
            for here, peak, acc in add_block(h, j, first):
                peaks[here, :] = peak
                sums[here, :] = acc

        each_group(body)

    def last_block(h):
        def body(first):
            for t, (here, _, acc) in enumerate(add_block(h, 0, first)):
                position = (
                    first + t * query_tile + lax.broadcasted_iota(jnp.int32, (query_tile, HD), 0)
                )
                value = jnp.where(
                    position < lengths_ref[span], acc[:, :HD] / acc[:, HD:], 0.0
                )
                results[h, here, :] = value.astype(jnp.bfloat16)

            def start_result(i, carry):
                rank = first // rows + i

                @pl.when(rank != me)
                def _():
                    send_result(h, rank).start()

                @pl.when(rank == me)
                def _():
                    pltpu.make_async_copy(
                        results.at[h, block_rows(me), :],
                        out_ref.at[0, :, columns(me, h)],
                        result_recv.at[h, me],
                    ).start()

                return carry

            lax.fori_loop(0, side * query_tile // rows, start_result, 0)

        each_group(body)

    read_lengths.wait()
    pass_near(0)
    advance()
    for h in range(heads):
        pass_far(h, span)

        @pl.when(span > 0)
        def _(h=h):
            pass_far(h, span - 1)

        advance()
        if h + 1 < heads:

            @pl.when(span < spans - 1)
            def _(h=h):
                pass_near(h + 1)

        start_state()
        wait_queries(h)

        def step(i, carry, h=h):
            middle_block(h, span - i)

            @pl.when(i + 1 < span)
            def _():
                pass_far(h, span - i - 2)

            return carry

        lax.fori_loop(0, span, step, 0)
        last_block(h)
        if h + 1 < heads:

            @pl.when(span == spans - 1)
            def _(h=h):
                pass_near(h + 1)

    for group in in_flight:
        drain_group(*group)

    for h in range(heads):

        def finish(i, carry, h=h):
            rank = lax.rem(me + i, ranks)
            send_result(h, rank).wait_send()
            return carry

        lax.fori_loop(1, ranks, finish, 0)

        @pl.when(span < spans - 1)
        def _(h=h):
            def finish_rank(rank, carry):
                def finish_span(j, carry):
                    forward(h, rank, j).wait_send()
                    return carry

                return lax.fori_loop(0, span + 1, finish_span, carry)

            lax.fori_loop(0, ranks, finish_rank, 0)

        def arrived(rank, carry, h=h):
            wait_bytes(out_ref.at[0, :, columns(rank, h)], result_recv.at[h, rank])
            return carry

        lax.fori_loop(0, ranks, arrived, 0)


def shards(spans, ranks, qkv, lengths):
    rows, features = qkv.shape[2], qkv.shape[3]
    heads = features // HD // ranks
    tokens = rows * ranks
    dma = pltpu.SemaphoreType.DMA
    return pl.pallas_call(
        functools.partial(kernel, spans, ranks, heads, rows),
        out_shape=jax.ShapeDtypeStruct((1, rows, features), jnp.bfloat16),
        in_specs=[
            pl.BlockSpec(memory_space=pltpu.HBM),
            pl.BlockSpec(memory_space=pltpu.HBM),
        ],
        out_specs=pl.BlockSpec(memory_space=pl.ANY),
        scratch_shapes=[
            pltpu.VMEM((heads, 2, spans, tokens, HD), jnp.bfloat16),
            pltpu.VMEM((heads, tokens, HD), jnp.bfloat16),
            pltpu.VMEM((heads, tokens, HD), jnp.bfloat16),
            pltpu.VMEM((tokens, 1), jnp.float32),
            pltpu.VMEM((tokens, 2 * HD), jnp.float32),
            pltpu.SMEM((spans,), jnp.int32),
            dma(()),
            dma((heads, ranks)),
            dma((heads, ranks)),
            dma((heads, ranks)),
            dma((heads, ranks, spans)),
            dma((heads, ranks, spans)),
            dma((heads, ranks)),
            dma((heads, ranks)),
        ],
        compiler_params=pltpu.CompilerParams(
            collective_id=0, has_side_effects=True, vmem_limit_bytes=64 * 2**20
        ),
    )(lengths, qkv)


def solution(mesh):
    in_specs = (P(None, "span", "seq", None), P())
    out_specs = P("span", "seq", None)
    body = functools.partial(shards, mesh.shape["span"], mesh.shape["seq"])
    return jax.shard_map(body, mesh=mesh, in_specs=in_specs, out_specs=out_specs, check_vma=False)
```

```python
import functools

import jax
import jax.numpy as jnp
from jax import lax
from jax.experimental import pallas as pl
from jax.experimental.pallas import tpu as pltpu
from jax.sharding import PartitionSpec as P

HD = 128
MASKED = -1e30
LOG2E = 1.4426950408889634
MESH = pl.DeviceIdType.MESH


def kernel(
    spans, ranks, heads, rows, lengths_hbm, qkv_ref, out_ref,
    keys, queries, results,  lengths_ref, lengths_sem,
    pair_send, query_send, result_send, forward_send,
    pair_recv, query_recv, result_recv,
):
    span = lax.axis_index("span")
    me = lax.axis_index("seq")
    tokens = rows * ranks
    half = ranks // 2
    query_tile = min(256, half * rows)

    barrier = pltpu.get_barrier_semaphore()

    def greet(k, carry):
        pl.semaphore_signal(
            barrier, inc=1, device_id=(span, lax.rem(me + k, ranks)), device_id_type=MESH
        )
        return carry

    lax.fori_loop(1, ranks, greet, 0)

    @pl.when(span > 0)
    def _():
        pl.semaphore_signal(barrier, inc=1, device_id=(span - 1, me), device_id_type=MESH)

    @pl.when(span < spans - 1)
    def _():
        pl.semaphore_signal(barrier, inc=1, device_id=(span + 1, me), device_id_type=MESH)

    def block_rows(rank):
        return pl.ds(pl.multiple_of(rank * rows, rows), rows)

    def columns(rank, h):
        return pl.ds(pl.multiple_of((rank * heads + h) * HD, HD), HD)

    def pair_slot(h, rank, j):
        return keys.at[h, :, j, block_rows(rank), :]

    def query_slot(h, rank):
        return queries.at[h, block_rows(rank), :]

    def partner(k):
        total = 0
        for bit in range(ranks.bit_length() - 1):
            unit = 2**bit
            total += lax.rem(me // unit + k // unit, 2) * unit
        return total

    def send_step(i):
        odd = lax.rem(i, 2)
        return odd * ((i + 1) // 2) + (1 - odd) * (half + i // 2)

    def pair_source(rank, h):
        return qkv_ref.at[pl.ds(1, 2), 0, :, columns(rank, h)]

    def query_source(rank, h):
        return qkv_ref.at[0, 0, :, columns(rank, h)]

    def own_pair(h):
        return pltpu.make_async_copy(
            pair_source(me, h), pair_slot(h, me, span), pair_recv.at[h, me, span]
        )

    def own_query(h):
        return pltpu.make_async_copy(
            query_source(me, h), query_slot(h, me), query_recv.at[h, me]
        )

    def send_pair(h, rank):
        return pltpu.make_async_remote_copy(
            src_ref=pair_source(rank, h),
            dst_ref=pair_slot(h, me, span),
            send_sem=pair_send.at[h, rank],
            recv_sem=pair_recv.at[h, me, span],
            device_id=(span, rank),
            device_id_type=MESH,
        )

    def send_query(h, rank):
        return pltpu.make_async_remote_copy(
            src_ref=query_source(rank, h),
            dst_ref=query_slot(h, me),
            send_sem=query_send.at[h, rank],
            recv_sem=query_recv.at[h, me],
            device_id=(span, rank),
            device_id_type=MESH,
        )

    def send_result(h, rank):
        return pltpu.make_async_remote_copy(
            src_ref=results.at[h, block_rows(rank), :],
            dst_ref=out_ref.at[0, :, columns(me, h)],
            send_sem=result_send.at[h, rank],
            recv_sem=result_recv.at[h, me],
            device_id=(span, rank),
            device_id_type=MESH,
        )

    def forward(h, rank, j):
        return pltpu.make_async_remote_copy(
            src_ref=pair_slot(h, rank, j),
            dst_ref=pair_slot(h, rank, j),
            send_sem=forward_send.at[h, rank, j],
            recv_sem=pair_recv.at[h, rank, j],
            device_id=(span + 1, me),
            device_id_type=MESH,
        )

    def wait_bytes(ref, sem):
        pltpu.make_async_copy(ref, ref, sem).wait()

    read_lengths = pltpu.make_async_copy(lengths_hbm, lengths_ref, lengths_sem)
    read_lengths.start()
    for h in range(heads):
        own_pair(h).start()
        own_query(h).start()

    pl.semaphore_wait(
        barrier,
        ranks - 1 + (span > 0).astype(jnp.int32) + (span < spans - 1).astype(jnp.int32),
    )

    groups = [(h, make) for make in (send_pair, send_query) for h in range(heads)]
    in_flight = []

    def start_group(h, make):
        def step(i, carry):
            make(h, partner(send_step(i))).start()
            return carry

        lax.fori_loop(0, ranks - 1, step, 0)

    def drain_group(h, make):
        def step(i, carry):
            make(h, partner(send_step(i))).wait_send()
            return carry

        lax.fori_loop(0, ranks - 1, step, 0)

    def advance():
        if groups:
            if len(in_flight) == 2:
                drain_group(*in_flight.pop(0))
            in_flight.append(groups.pop(0))
            start_group(*in_flight[-1])

    advance()
    advance()

    def pass_on(h, j, first, last):
        def step(k, carry):
            rank = partner(k)
            wait_bytes(pair_slot(h, rank, j), pair_recv.at[h, rank, j])

            @pl.when(span < spans - 1)
            def _():
                forward(h, rank, j).start()

            return carry

        lax.fori_loop(first, last, step, 0)

    def pass_near(h):
        def step(i, carry):
            pass_on(h, span - i, 0, half)
            return carry

        lax.fori_loop(0, span + 1, step, 0)

    def pass_far(h, j):
        pass_on(h, j, half, ranks)

    ones = jnp.ones((tokens, HD), jnp.bfloat16)

    def attend(h, first_rank):
        def wait_query(i, carry):
            rank = first_rank + i
            wait_bytes(query_slot(h, rank), query_recv.at[h, rank])
            return carry

        lax.fori_loop(0, half, wait_query, 0)

        def one_tile(tile, carry):
            first = pl.multiple_of(first_rank * rows + tile * query_tile, query_tile)
            here = pl.ds(first, query_tile)
            q = queries[h, here, :]

            def add_block(j, state):
                peak, acc = state
                live = lax.broadcasted_iota(jnp.int32, (1, tokens), 1) < lengths_ref[j]
                limit = jnp.where(live, -2 * MASKED, MASKED)
                scores = lax.dot_general(
                    q, keys[h, 0, j], (((1,), (1,)), ((), ())), preferred_element_type=jnp.float32
                )
                scores = jnp.minimum(scores, limit)
                new_peak = jnp.maximum(peak, jnp.max(scores, axis=1, keepdims=True))
                weights = jnp.exp2((scores - new_peak) * (LOG2E * HD**-0.5)).astype(jnp.bfloat16)
                scale = jnp.exp2((peak - new_peak) * (LOG2E * HD**-0.5))
                v = jnp.concatenate([keys[h, 1, j], ones], axis=1)
                acc = acc * scale + jnp.dot(weights, v, preferred_element_type=jnp.float32)
                return new_peak, acc

            _, acc = lax.fori_loop(
                0,
                span + 1,
                add_block,
                (
                    jnp.full((query_tile, 1), MASKED, jnp.float32),
                    jnp.zeros((query_tile, 2 * HD), jnp.float32),
                ),
            )
            position = first + lax.broadcasted_iota(jnp.int32, (query_tile, HD), 0)
            value = jnp.where(position < lengths_ref[span], acc[:, :HD] / acc[:, HD:], 0.0)
            results[h, here, :] = value.astype(jnp.bfloat16)

            def start_result(i, carry):
                rank = first_rank + tile * (query_tile // rows) + i

                @pl.when(rank != me)
                def _():
                    send_result(h, rank).start()

                @pl.when(rank == me)
                def _():
                    pltpu.make_async_copy(
                        results.at[h, block_rows(me), :],
                        out_ref.at[0, :, columns(me, h)],
                        result_recv.at[h, me],
                    ).start()

                return carry

            lax.fori_loop(0, query_tile // rows, start_result, 0)
            return carry

        lax.fori_loop(0, half * rows // query_tile, one_tile, 0)

    near = me // half * half
    far = half - near

    read_lengths.wait()
    for h in range(heads):
        pass_near(h)
    advance()
    for h in range(heads):

        def step(i, carry, h=h):
            pass_far(h, span - i)
            return carry

        lax.fori_loop(0, span + 1, step, 0)
        attend(h, near)
        advance()
    for h in range(heads):
        attend(h, far)

    for group in in_flight:
        drain_group(*group)

    for h in range(heads):

        def finish(i, carry, h=h):
            rank = lax.rem(me + i, ranks)
            send_result(h, rank).wait_send()
            return carry

        lax.fori_loop(1, ranks, finish, 0)

        @pl.when(span < spans - 1)
        def _(h=h):
            def finish_rank(rank, carry):
                def finish_span(j, carry):
                    forward(h, rank, j).wait_send()
                    return carry

                return lax.fori_loop(0, span + 1, finish_span, carry)

            lax.fori_loop(0, ranks, finish_rank, 0)

        def arrived(rank, carry, h=h):
            wait_bytes(out_ref.at[0, :, columns(rank, h)], result_recv.at[h, rank])
            return carry

        lax.fori_loop(0, ranks, arrived, 0)


def shards(spans, ranks, qkv, lengths):
    rows, features = qkv.shape[2], qkv.shape[3]
    heads = features // HD // ranks
    tokens = rows * ranks
    dma = pltpu.SemaphoreType.DMA
    attended = pl.pallas_call(
        functools.partial(kernel, spans, ranks, heads, rows),
        out_shape=jax.ShapeDtypeStruct((1, rows, features), jnp.bfloat16),
        in_specs=[
            pl.BlockSpec(memory_space=pltpu.HBM),
            pl.BlockSpec(memory_space=pltpu.HBM),
        ],
        out_specs=pl.BlockSpec(memory_space=pl.ANY),
        scratch_shapes=[
            pltpu.VMEM((heads, 2, spans, tokens, HD), jnp.bfloat16),
            pltpu.VMEM((heads, tokens, HD), jnp.bfloat16),
            pltpu.VMEM((heads, tokens, HD), jnp.bfloat16),
            pltpu.SMEM((spans,), jnp.int32),
            dma(()),
            dma((heads, ranks)),
            dma((heads, ranks)),
            dma((heads, ranks)),
            dma((heads, ranks, spans)),
            dma((heads, ranks, spans)),
            dma((heads, ranks)),
            dma((heads, ranks)),
        ],
        compiler_params=pltpu.CompilerParams(
            collective_id=0, has_side_effects=True, vmem_limit_bytes=64 * 2**20
        ),
    )(lengths, qkv)
    return jnp.maximum(attended, jnp.finfo(jnp.bfloat16).min)


def solution(mesh):
    in_specs = (P(None, "span", "seq", None), P())
    out_specs = P("span", "seq", None)
    body = functools.partial(shards, mesh.shape["span"], mesh.shape["seq"])
    return jax.shard_map(body, mesh=mesh, in_specs=in_specs, out_specs=out_specs, check_vma=False)
```

```python
import functools

import jax
import jax.numpy as jnp
from jax import lax
from jax.experimental import pallas as pl
from jax.experimental.pallas import tpu as pltpu
from jax.sharding import PartitionSpec as P

HD = 128
MASKED = -1e30
LOG2E = 1.4426950408889634
MESH = pl.DeviceIdType.MESH


def kernel(
    spans, ranks, heads, rows, lengths_hbm, qkv_ref, out_ref,
    keys, queries, results, peaks, totals, sums, lengths_ref, lengths_sem,
    pair_send, query_send, result_send, forward_send,
    pair_recv, query_recv, result_recv,
):
    span = lax.axis_index("span")
    me = lax.axis_index("seq")
    tokens = rows * ranks
    query_tile = min(256, tokens)
    half = ranks // 2

    barrier = pltpu.get_barrier_semaphore()

    def greet(k, carry):
        pl.semaphore_signal(
            barrier, inc=1, device_id=(span, lax.rem(me + k, ranks)), device_id_type=MESH
        )
        return carry

    lax.fori_loop(1, ranks, greet, 0)

    @pl.when(span > 0)
    def _():
        pl.semaphore_signal(barrier, inc=1, device_id=(span - 1, me), device_id_type=MESH)

    @pl.when(span < spans - 1)
    def _():
        pl.semaphore_signal(barrier, inc=1, device_id=(span + 1, me), device_id_type=MESH)

    def block_rows(rank):
        return pl.ds(pl.multiple_of(rank * rows, rows), rows)

    def columns(rank, h):
        return pl.ds(pl.multiple_of((rank * heads + h) * HD, HD), HD)

    def pair_slot(h, rank, j):
        return keys.at[h, :, j, block_rows(rank), :]

    def query_slot(h, rank):
        return queries.at[h, block_rows(rank), :]

    def partner(k):
        total = 0
        for bit in range(ranks.bit_length() - 1):
            unit = 2**bit
            total += lax.rem(me // unit + k // unit, 2) * unit
        return total

    def send_step(i):
        odd = lax.rem(i, 2)
        return odd * ((i + 1) // 2) + (1 - odd) * (half + i // 2)

    def pair_source(rank, h):
        return qkv_ref.at[pl.ds(1, 2), 0, :, columns(rank, h)]

    def query_source(rank, h):
        return qkv_ref.at[0, 0, :, columns(rank, h)]

    def own_pair(h):
        return pltpu.make_async_copy(
            pair_source(me, h), pair_slot(h, me, span), pair_recv.at[h, me, span]
        )

    def own_query(h):
        return pltpu.make_async_copy(
            query_source(me, h), query_slot(h, me), query_recv.at[h, me]
        )

    def send_pair(h, rank):
        return pltpu.make_async_remote_copy(
            src_ref=pair_source(rank, h),
            dst_ref=pair_slot(h, me, span),
            send_sem=pair_send.at[h, rank],
            recv_sem=pair_recv.at[h, me, span],
            device_id=(span, rank),
            device_id_type=MESH,
        )

    def send_query(h, rank):
        return pltpu.make_async_remote_copy(
            src_ref=query_source(rank, h),
            dst_ref=query_slot(h, me),
            send_sem=query_send.at[h, rank],
            recv_sem=query_recv.at[h, me],
            device_id=(span, rank),
            device_id_type=MESH,
        )

    def send_result(h, rank):
        return pltpu.make_async_remote_copy(
            src_ref=results.at[h, block_rows(rank), :],
            dst_ref=out_ref.at[0, :, columns(me, h)],
            send_sem=result_send.at[h, rank],
            recv_sem=result_recv.at[h, me],
            device_id=(span, rank),
            device_id_type=MESH,
        )

    def forward(h, rank, j):
        return pltpu.make_async_remote_copy(
            src_ref=pair_slot(h, rank, j),
            dst_ref=pair_slot(h, rank, j),
            send_sem=forward_send.at[h, rank, j],
            recv_sem=pair_recv.at[h, rank, j],
            device_id=(span + 1, me),
            device_id_type=MESH,
        )

    def wait_bytes(ref, sem):
        pltpu.make_async_copy(ref, ref, sem).wait()

    read_lengths = pltpu.make_async_copy(lengths_hbm, lengths_ref, lengths_sem)
    read_lengths.start()
    for h in range(heads):
        own_pair(h).start()
        own_query(h).start()

    pl.semaphore_wait(
        barrier,
        ranks - 1 + (span > 0).astype(jnp.int32) + (span < spans - 1).astype(jnp.int32),
    )

    def start_group(h, make):
        def step(i, carry):
            make(h, partner(send_step(i))).start()
            return carry

        lax.fori_loop(0, ranks - 1, step, 0)

    def drain_group(h, make):
        def step(i, carry):
            make(h, partner(send_step(i))).wait_send()
            return carry

        lax.fori_loop(0, ranks - 1, step, 0)

    early = span < (spans + 1) // 2
    late = jnp.logical_not(early)
    orders = (
        (early, [(h, make) for make in (send_pair, send_query) for h in range(heads)]),
        (late, [(h, make) for h in range(heads) for make in (send_query, send_pair)]),
    )
    ahead = min(3, 2 * heads)
    for here, order in orders:

        @pl.when(here)
        def _(order=order):
            for group in order[:ahead]:
                start_group(*group)

    def send_rest(order):
        for i in range(ahead, 2 * heads):
            drain_group(*order[i - ahead])
            start_group(*order[i])

    def drain_rest(order):
        for group in order[max(0, 2 * heads - ahead) :]:
            drain_group(*group)

    def pass_on(h, j, first, last):
        def step(k, carry):
            rank = partner(k)
            wait_bytes(pair_slot(h, rank, j), pair_recv.at[h, rank, j])

            @pl.when(span < spans - 1)
            def _():
                forward(h, rank, j).start()

            return carry

        lax.fori_loop(first, last, step, 0)

    def pass_near(h):
        def step(i, carry):
            pass_on(h, span - i, 0, half)
            return carry

        lax.fori_loop(0, span + 1, step, 0)

    def pass_far(h, j):
        pass_on(h, j, half, ranks)

    def wait_queries(h):
        def step(rank, carry):
            wait_bytes(query_slot(h, rank), query_recv.at[h, rank])
            return carry

        lax.fori_loop(0, ranks, step, 0)

    def add_block(h, j, here, live):
        scores = lax.dot_general(
            queries[h, here, :],
            keys[h, 0, j],
            (((1,), (1,)), ((), ())),
            preferred_element_type=jnp.float32,
        )
        position = lax.broadcasted_iota(jnp.int32, (1, tokens), 1)
        scores = jnp.minimum(scores, jnp.where(position < live, -2 * MASKED, MASKED))
        peak = peaks[here, :]
        new_peak = jnp.maximum(peak, jnp.max(scores, axis=1, keepdims=True))
        weights = jnp.exp2((scores - new_peak) * (LOG2E * HD**-0.5)).astype(jnp.bfloat16)
        scale = jnp.exp2((peak - new_peak) * (LOG2E * HD**-0.5))
        total = totals[here, :] * scale + jnp.sum(
            weights.astype(jnp.float32), axis=1, keepdims=True
        )
        acc = sums[here, :] * scale + jnp.dot(
            weights, keys[h, 1, j], preferred_element_type=jnp.float32
        )
        return new_peak, total, acc

    def tile_rows(tile):
        return pl.ds(pl.multiple_of(tile * query_tile, query_tile), query_tile)

    tiles = tokens // query_tile

    def start_state():
        peaks[...] = jnp.full(peaks.shape, MASKED, jnp.float32)
        totals[...] = jnp.zeros(totals.shape, jnp.float32)
        sums[...] = jnp.zeros(sums.shape, jnp.float32)

    def middle_block(h, j):
        def one_tile(tile, carry):
            here = tile_rows(tile)
            peaks[here, :], totals[here, :], sums[here, :] = add_block(
                h, j, here, lengths_ref[j]
            )
            return carry

        lax.fori_loop(0, tiles, one_tile, 0)

    def last_block(h):
        def one_tile(tile, carry):
            here = tile_rows(tile)
            _, total, acc = add_block(h, span, here, lengths_ref[span])
            position = tile * query_tile + lax.broadcasted_iota(jnp.int32, acc.shape, 0)
            value = jnp.where(position < lengths_ref[span], acc / total, 0.0)
            results[h, here, :] = value.astype(jnp.bfloat16)

            def start_result(i, carry):
                rank = tile * (query_tile // rows) + i

                @pl.when(rank != me)
                def _():
                    send_result(h, rank).start()

                @pl.when(rank == me)
                def _():
                    pltpu.make_async_copy(
                        results.at[h, block_rows(me), :],
                        out_ref.at[0, :, columns(me, h)],
                        result_recv.at[h, me],
                    ).start()

                return carry

            lax.fori_loop(0, query_tile // rows, start_result, 0)
            return carry

        lax.fori_loop(0, tiles, one_tile, 0)

    def compute_head(h, waits):
        wait_queries(h)
        start_state()

        def step(j, carry):
            if waits:
                pass_far(h, j + 1)
            middle_block(h, j)
            return carry

        lax.fori_loop(0, span, step, 0)
        last_block(h)

    read_lengths.wait()

    @pl.when(early)
    def _():
        for h in range(heads):
            pass_near(h)
        send_rest(orders[0][1])
        for h in range(heads):

            def step(i, carry, h=h):
                pass_far(h, span - i)
                return carry

            lax.fori_loop(0, span + 1, step, 0)
        for h in range(heads):
            compute_head(h, False)
        drain_rest(orders[0][1])

    @pl.when(late)
    def _():
        send_rest(orders[1][1])
        for h in range(heads):
            pass_near(h)
            pass_far(h, 0)
            compute_head(h, True)
        drain_rest(orders[1][1])

    for h in range(heads):

        def finish(i, carry, h=h):
            rank = lax.rem(me + i, ranks)
            send_result(h, rank).wait_send()
            return carry

        lax.fori_loop(1, ranks, finish, 0)

        @pl.when(span < spans - 1)
        def _(h=h):
            def finish_rank(rank, carry):
                def finish_span(j, carry):
                    forward(h, rank, j).wait_send()
                    return carry

                return lax.fori_loop(0, span + 1, finish_span, carry)

            lax.fori_loop(0, ranks, finish_rank, 0)

        def arrived(rank, carry, h=h):
            wait_bytes(out_ref.at[0, :, columns(rank, h)], result_recv.at[h, rank])
            return carry

        lax.fori_loop(0, ranks, arrived, 0)


def shards(spans, ranks, qkv, lengths):
    rows, features = qkv.shape[2], qkv.shape[3]
    heads = features // HD // ranks
    tokens = rows * ranks
    dma = pltpu.SemaphoreType.DMA
    return pl.pallas_call(
        functools.partial(kernel, spans, ranks, heads, rows),
        out_shape=jax.ShapeDtypeStruct((1, rows, features), jnp.bfloat16),
        in_specs=[
            pl.BlockSpec(memory_space=pltpu.HBM),
            pl.BlockSpec(memory_space=pltpu.HBM),
        ],
        out_specs=pl.BlockSpec(memory_space=pl.ANY),
        scratch_shapes=[
            pltpu.VMEM((heads, 2, spans, tokens, HD), jnp.bfloat16),
            pltpu.VMEM((heads, tokens, HD), jnp.bfloat16),
            pltpu.VMEM((heads, tokens, HD), jnp.bfloat16),
            pltpu.VMEM((tokens, 1), jnp.float32),
            pltpu.VMEM((tokens, 1), jnp.float32),
            pltpu.VMEM((tokens, HD), jnp.float32),
            pltpu.SMEM((spans,), jnp.int32),
            dma(()),
            dma((heads, ranks)),
            dma((heads, ranks)),
            dma((heads, ranks)),
            dma((heads, ranks, spans)),
            dma((heads, ranks, spans)),
            dma((heads, ranks)),
            dma((heads, ranks)),
        ],
        compiler_params=pltpu.CompilerParams(
            collective_id=0, has_side_effects=True, vmem_limit_bytes=64 * 2**20
        ),
    )(lengths, qkv)


def solution(mesh):
    in_specs = (P(None, "span", "seq", None), P())
    out_specs = P("span", "seq", None)
    body = functools.partial(shards, mesh.shape["span"], mesh.shape["seq"])
    return jax.shard_map(body, mesh=mesh, in_specs=in_specs, out_specs=out_specs, check_vma=False)
```

```python
import functools

import jax
import jax.numpy as jnp
from jax import lax
from jax.experimental import pallas as pl
from jax.experimental.pallas import tpu as pltpu
from jax.sharding import PartitionSpec as P

HD = 128
MASKED = -1e30
LOG2E = 1.4426950408889634
MESH = pl.DeviceIdType.MESH


def kernel(
    spans, ranks, heads, rows, lengths_hbm, qkv_ref, out_ref,
    keys, queries, results, peaks, sums, lengths_ref, lengths_sem,
    pair_send, query_send, result_send, forward_send,
    pair_recv, query_recv, result_recv,
):
    span = lax.axis_index("span")
    me = lax.axis_index("seq")
    tokens = rows * ranks
    query_tile = min(256, tokens)
    half = ranks // 2

    barrier = pltpu.get_barrier_semaphore()

    def greet(k, carry):
        pl.semaphore_signal(
            barrier, inc=1, device_id=(span, lax.rem(me + k, ranks)), device_id_type=MESH
        )
        return carry

    lax.fori_loop(1, ranks, greet, 0)

    @pl.when(span > 0)
    def _():
        pl.semaphore_signal(barrier, inc=1, device_id=(span - 1, me), device_id_type=MESH)

    @pl.when(span < spans - 1)
    def _():
        pl.semaphore_signal(barrier, inc=1, device_id=(span + 1, me), device_id_type=MESH)

    def block_rows(rank):
        return pl.ds(pl.multiple_of(rank * rows, rows), rows)

    def columns(rank, h):
        return pl.ds(pl.multiple_of((rank * heads + h) * HD, HD), HD)

    def pair_slot(h, rank, j):
        return keys.at[h, :, j, block_rows(rank), :]

    def query_slot(h, rank):
        return queries.at[h, block_rows(rank), :]

    def partner(k):
        total = 0
        for bit in range(ranks.bit_length() - 1):
            unit = 2**bit
            total += lax.rem(me // unit + k // unit, 2) * unit
        return total

    def send_step(i):
        odd = lax.rem(i, 2)
        return odd * ((i + 1) // 2) + (1 - odd) * (half + i // 2)

    def pair_source(rank, h):
        return qkv_ref.at[pl.ds(1, 2), 0, :, columns(rank, h)]

    def query_source(rank, h):
        return qkv_ref.at[0, 0, :, columns(rank, h)]

    def own_pair(h):
        return pltpu.make_async_copy(
            pair_source(me, h), pair_slot(h, me, span), pair_recv.at[h, me, span]
        )

    def own_query(h):
        return pltpu.make_async_copy(
            query_source(me, h), query_slot(h, me), query_recv.at[h, me]
        )

    def send_pair(h, rank):
        return pltpu.make_async_remote_copy(
            src_ref=pair_source(rank, h),
            dst_ref=pair_slot(h, me, span),
            send_sem=pair_send.at[h, rank],
            recv_sem=pair_recv.at[h, me, span],
            device_id=(span, rank),
            device_id_type=MESH,
        )

    def send_query(h, rank):
        return pltpu.make_async_remote_copy(
            src_ref=query_source(rank, h),
            dst_ref=query_slot(h, me),
            send_sem=query_send.at[h, rank],
            recv_sem=query_recv.at[h, me],
            device_id=(span, rank),
            device_id_type=MESH,
        )

    def send_result(h, rank):
        return pltpu.make_async_remote_copy(
            src_ref=results.at[h, block_rows(rank), :],
            dst_ref=out_ref.at[0, :, columns(me, h)],
            send_sem=result_send.at[h, rank],
            recv_sem=result_recv.at[h, me],
            device_id=(span, rank),
            device_id_type=MESH,
        )

    def forward(h, rank, j):
        return pltpu.make_async_remote_copy(
            src_ref=pair_slot(h, rank, j),
            dst_ref=pair_slot(h, rank, j),
            send_sem=forward_send.at[h, rank, j],
            recv_sem=pair_recv.at[h, rank, j],
            device_id=(span + 1, me),
            device_id_type=MESH,
        )

    def wait_bytes(ref, sem):
        pltpu.make_async_copy(ref, ref, sem).wait()

    read_lengths = pltpu.make_async_copy(lengths_hbm, lengths_ref, lengths_sem)
    read_lengths.start()
    for h in range(heads):
        own_pair(h).start()
        own_query(h).start()

    pl.semaphore_wait(
        barrier,
        ranks - 1 + (span > 0).astype(jnp.int32) + (span < spans - 1).astype(jnp.int32),
    )

    groups = [(h, make) for h in range(heads) for make in (send_pair, send_query)]
    in_flight = []

    def start_group(h, make):
        def step(i, carry):
            make(h, partner(send_step(i))).start()
            return carry

        lax.fori_loop(0, ranks - 1, step, 0)

    def drain_group(h, make):
        def step(i, carry):
            make(h, partner(send_step(i))).wait_send()
            return carry

        lax.fori_loop(0, ranks - 1, step, 0)

    def advance():
        if groups:
            if len(in_flight) == 2:
                drain_group(*in_flight.pop(0))
            in_flight.append(groups.pop(0))
            start_group(*in_flight[-1])

    advance()
    advance()

    def pass_on(h, j, first, last):
        def step(k, carry):
            rank = partner(k)
            wait_bytes(pair_slot(h, rank, j), pair_recv.at[h, rank, j])

            @pl.when(span < spans - 1)
            def _():
                forward(h, rank, j).start()

            return carry

        lax.fori_loop(first, last, step, 0)

    def pass_near(h):
        pass_on(h, span, 0, half)
        advance()

        def step(i, carry):
            pass_on(h, span - i, 0, half)
            return carry

        lax.fori_loop(1, span + 1, step, 0)

    def pass_far(h, j):
        pass_on(h, j, half, ranks)

    def wait_queries(h):
        def step(rank, carry):
            wait_bytes(query_slot(h, rank), query_recv.at[h, rank])
            return carry

        lax.fori_loop(0, ranks, step, 0)

    ones = jnp.ones((16, tokens), jnp.bfloat16)

    def add_block(h, j):
        k = keys[h, 0, j]
        v = jnp.concatenate([keys[h, 1, j].T, ones], axis=0)
        live = lax.broadcasted_iota(jnp.int32, (tokens, query_tile), 0) < lengths_ref[j]
        states = []
        for first in range(0, tokens, query_tile):
            here = pl.ds(first, query_tile)
            scores = lax.dot_general(
                k,
                queries[h, here, :],
                (((1,), (1,)), ((), ())),
                preferred_element_type=jnp.float32,
            )
            scores = jnp.where(live, scores, MASKED)
            peak = peaks[:, here]
            new_peak = jnp.maximum(peak, jnp.max(scores, axis=0, keepdims=True))
            weights = jnp.exp2((scores - new_peak) * (LOG2E * HD**-0.5)).astype(jnp.bfloat16)
            scale = jnp.exp2((peak - new_peak) * (LOG2E * HD**-0.5))
            acc = sums[:, here] * scale + jnp.dot(v, weights, preferred_element_type=jnp.float32)
            states.append((here, new_peak, acc))
        return states

    def start_state():
        peaks[...] = jnp.full(peaks.shape, MASKED, jnp.float32)
        sums[...] = jnp.zeros(sums.shape, jnp.float32)

    def middle_block(h, j):
        for here, peak, acc in add_block(h, j):
            peaks[:, here] = peak
            sums[:, here] = acc

    def last_block(h):
        for here, _, acc in add_block(h, 0):
            position = here.start + lax.broadcasted_iota(jnp.int32, (HD, query_tile), 1)
            value = jnp.where(position < lengths_ref[span], acc[:HD] / acc[HD : HD + 1], 0.0)
            results[h, here, :] = value.T.astype(jnp.bfloat16)

        def start_result(rank, carry):
            @pl.when(rank != me)
            def _():
                send_result(h, rank).start()

            @pl.when(rank == me)
            def _():
                pltpu.make_async_copy(
                    results.at[h, block_rows(me), :],
                    out_ref.at[0, :, columns(me, h)],
                    result_recv.at[h, me],
                ).start()

            return carry

        lax.fori_loop(0, ranks, start_result, 0)

    read_lengths.wait()
    pass_near(0)
    for h in range(heads):
        start_state()
        pass_far(h, span)
        advance()

        @pl.when(span > 0)
        def _(h=h):
            pass_far(h, span - 1)

        wait_queries(h)

        def step(i, carry, h=h):
            middle_block(h, span - i)

            @pl.when(i + 1 < span)
            def _():
                pass_far(h, span - i - 2)

            return carry

        lax.fori_loop(0, span, step, 0)
        if h + 1 < heads:
            pass_near(h + 1)
        last_block(h)

    for group in in_flight:
        drain_group(*group)

    for h in range(heads):

        def finish(i, carry, h=h):
            rank = lax.rem(me + i, ranks)
            send_result(h, rank).wait_send()
            return carry

        lax.fori_loop(1, ranks, finish, 0)

        @pl.when(span < spans - 1)
        def _(h=h):
            def finish_rank(rank, carry):
                def finish_span(j, carry):
                    forward(h, rank, j).wait_send()
                    return carry

                return lax.fori_loop(0, span + 1, finish_span, carry)

            lax.fori_loop(0, ranks, finish_rank, 0)

        def arrived(rank, carry, h=h):
            wait_bytes(out_ref.at[0, :, columns(rank, h)], result_recv.at[h, rank])
            return carry

        lax.fori_loop(0, ranks, arrived, 0)


def shards(spans, ranks, qkv, lengths):
    rows, features = qkv.shape[2], qkv.shape[3]
    heads = features // HD // ranks
    tokens = rows * ranks
    dma = pltpu.SemaphoreType.DMA
    return pl.pallas_call(
        functools.partial(kernel, spans, ranks, heads, rows),
        out_shape=jax.ShapeDtypeStruct((1, rows, features), jnp.bfloat16),
        in_specs=[
            pl.BlockSpec(memory_space=pltpu.HBM),
            pl.BlockSpec(memory_space=pltpu.HBM),
        ],
        out_specs=pl.BlockSpec(memory_space=pl.ANY),
        scratch_shapes=[
            pltpu.VMEM((heads, 2, spans, tokens, HD), jnp.bfloat16),
            pltpu.VMEM((heads, tokens, HD), jnp.bfloat16),
            pltpu.VMEM((heads, tokens, HD), jnp.bfloat16),
            pltpu.VMEM((1, tokens), jnp.float32),
            pltpu.VMEM((HD + 16, tokens), jnp.float32),
            pltpu.SMEM((spans,), jnp.int32),
            dma(()),
            dma((heads, ranks)),
            dma((heads, ranks)),
            dma((heads, ranks)),
            dma((heads, ranks, spans)),
            dma((heads, ranks, spans)),
            dma((heads, ranks)),
            dma((heads, ranks)),
        ],
        compiler_params=pltpu.CompilerParams(
            collective_id=0, has_side_effects=True, vmem_limit_bytes=64 * 2**20
        ),
    )(lengths, qkv)


def solution(mesh):
    in_specs = (P(None, "span", "seq", None), P())
    out_specs = P("span", "seq", None)
    body = functools.partial(shards, mesh.shape["span"], mesh.shape["seq"])
    return jax.shard_map(body, mesh=mesh, in_specs=in_specs, out_specs=out_specs, check_vma=False)
```

```python
import functools

import jax
import jax.numpy as jnp
from jax import lax
from jax.experimental import pallas as pl
from jax.experimental.pallas import tpu as pltpu
from jax.sharding import PartitionSpec as P

HD = 128
MASKED = -1e30
LOG2E = 1.4426950408889634
MESH = pl.DeviceIdType.MESH


def kernel(
    spans, ranks, heads, rows, lengths_hbm, qkv_ref, out_ref,
    keys, queries, results, peaks, sums, lengths_ref, lengths_sem,
    pair_send, query_send, result_send, forward_send,
    pair_recv, query_recv, result_recv,
):
    span = lax.axis_index("span")
    me = lax.axis_index("seq")
    tokens = rows * ranks
    query_tile = min(256, tokens)
    half = ranks // 2

    barrier = pltpu.get_barrier_semaphore()

    def greet(k, carry):
        pl.semaphore_signal(
            barrier, inc=1, device_id=(span, lax.rem(me + k, ranks)), device_id_type=MESH
        )
        return carry

    lax.fori_loop(1, ranks, greet, 0)

    @pl.when(span > 0)
    def _():
        pl.semaphore_signal(barrier, inc=1, device_id=(span - 1, me), device_id_type=MESH)

    @pl.when(span < spans - 1)
    def _():
        pl.semaphore_signal(barrier, inc=1, device_id=(span + 1, me), device_id_type=MESH)

    def block_rows(rank):
        return pl.ds(pl.multiple_of(rank * rows, rows), rows)

    def columns(rank, h):
        return pl.ds(pl.multiple_of((rank * heads + h) * HD, HD), HD)

    def pair_slot(h, rank, j):
        return keys.at[h, :, j, block_rows(rank), :]

    def query_slot(h, rank):
        return queries.at[h, block_rows(rank), :]

    def partner(k):
        total = 0
        for bit in range(ranks.bit_length() - 1):
            unit = 2**bit
            total += lax.rem(me // unit + k // unit, 2) * unit
        return total

    def send_step(i):
        odd = lax.rem(i, 2)
        return odd * ((i + 1) // 2) + (1 - odd) * (half + i // 2)

    def pair_source(rank, h):
        return qkv_ref.at[pl.ds(1, 2), 0, :, columns(rank, h)]

    def query_source(rank, h):
        return qkv_ref.at[0, 0, :, columns(rank, h)]

    def own_pair(h):
        return pltpu.make_async_copy(
            pair_source(me, h), pair_slot(h, me, span), pair_recv.at[h, me, span]
        )

    def own_query(h):
        return pltpu.make_async_copy(
            query_source(me, h), query_slot(h, me), query_recv.at[h, me]
        )

    def send_pair(h, rank):
        return pltpu.make_async_remote_copy(
            src_ref=pair_source(rank, h),
            dst_ref=pair_slot(h, me, span),
            send_sem=pair_send.at[h, rank],
            recv_sem=pair_recv.at[h, me, span],
            device_id=(span, rank),
            device_id_type=MESH,
        )

    def send_query(h, rank):
        return pltpu.make_async_remote_copy(
            src_ref=query_source(rank, h),
            dst_ref=query_slot(h, me),
            send_sem=query_send.at[h, rank],
            recv_sem=query_recv.at[h, me],
            device_id=(span, rank),
            device_id_type=MESH,
        )

    def send_result(h, rank):
        return pltpu.make_async_remote_copy(
            src_ref=results.at[h, block_rows(rank), :],
            dst_ref=out_ref.at[0, :, columns(me, h)],
            send_sem=result_send.at[h, rank],
            recv_sem=result_recv.at[h, me],
            device_id=(span, rank),
            device_id_type=MESH,
        )

    def forward(h, rank, j):
        return pltpu.make_async_remote_copy(
            src_ref=pair_slot(h, rank, j),
            dst_ref=pair_slot(h, rank, j),
            send_sem=forward_send.at[h, rank, j],
            recv_sem=pair_recv.at[h, rank, j],
            device_id=(span + 1, me),
            device_id_type=MESH,
        )

    def wait_bytes(ref, sem):
        pltpu.make_async_copy(ref, ref, sem).wait()

    read_lengths = pltpu.make_async_copy(lengths_hbm, lengths_ref, lengths_sem)
    read_lengths.start()
    for h in range(heads):
        own_pair(h).start()
        own_query(h).start()

    pl.semaphore_wait(
        barrier,
        ranks - 1 + (span > 0).astype(jnp.int32) + (span < spans - 1).astype(jnp.int32),
    )

    def start_group(h, make):
        def step(i, carry):
            make(h, partner(send_step(i))).start()
            return carry

        lax.fori_loop(0, ranks - 1, step, 0)

    def drain_group(h, make):
        def step(i, carry):
            make(h, partner(send_step(i))).wait_send()
            return carry

        lax.fori_loop(0, ranks - 1, step, 0)

    early = span < (spans + 1) // 2
    late = jnp.logical_not(early)
    orders = (
        (early, [(h, make) for make in (send_pair, send_query) for h in range(heads)]),
        (late, [(h, make) for h in range(heads) for make in (send_query, send_pair)]),
    )
    ahead = min(3, 2 * heads)
    for here, order in orders:

        @pl.when(here)
        def _(order=order):
            for group in order[:ahead]:
                start_group(*group)

    def send_rest(order):
        for i in range(ahead, 2 * heads):
            drain_group(*order[i - ahead])
            start_group(*order[i])

    def drain_rest(order):
        for group in order[max(0, 2 * heads - ahead) :]:
            drain_group(*group)

    def pass_on(h, j, first, last):
        def step(k, carry):
            rank = partner(k)
            wait_bytes(pair_slot(h, rank, j), pair_recv.at[h, rank, j])

            @pl.when(span < spans - 1)
            def _():
                forward(h, rank, j).start()

            return carry

        lax.fori_loop(first, last, step, 0)

    def pass_near(h):
        def step(i, carry):
            pass_on(h, span - i, 0, half)
            return carry

        lax.fori_loop(0, span + 1, step, 0)

    def pass_far(h, j):
        pass_on(h, j, half, ranks)

    def wait_queries(h):
        def step(rank, carry):
            wait_bytes(query_slot(h, rank), query_recv.at[h, rank])
            return carry

        lax.fori_loop(0, ranks, step, 0)

    ones = jnp.ones((16, tokens), jnp.bfloat16)

    def add_block(h, j):
        k = keys[h, 0, j]
        v = jnp.concatenate([keys[h, 1, j].T, ones], axis=0)
        live = lax.broadcasted_iota(jnp.int32, (tokens, query_tile), 0) < lengths_ref[j]
        states = []
        for first in range(0, tokens, query_tile):
            here = pl.ds(first, query_tile)
            scores = lax.dot_general(
                k,
                queries[h, here, :],
                (((1,), (1,)), ((), ())),
                preferred_element_type=jnp.float32,
            )
            scores = jnp.where(live, scores, MASKED)
            peak = peaks[:, here]
            new_peak = jnp.maximum(peak, jnp.max(scores, axis=0, keepdims=True))
            weights = jnp.exp2((scores - new_peak) * (LOG2E * HD**-0.5)).astype(jnp.bfloat16)
            scale = jnp.exp2((peak - new_peak) * (LOG2E * HD**-0.5))
            acc = sums[:, here] * scale + jnp.dot(v, weights, preferred_element_type=jnp.float32)
            states.append((here, new_peak, acc))
        return states

    def start_state():
        peaks[...] = jnp.full(peaks.shape, MASKED, jnp.float32)
        sums[...] = jnp.zeros(sums.shape, jnp.float32)

    def middle_block(h, j):
        for here, peak, acc in add_block(h, j):
            peaks[:, here] = peak
            sums[:, here] = acc

    def last_block(h):
        for here, _, acc in add_block(h, span):
            position = here.start + lax.broadcasted_iota(jnp.int32, (HD, query_tile), 1)
            value = jnp.where(position < lengths_ref[span], acc[:HD] / acc[HD : HD + 1], 0.0)
            results[h, here, :] = value.T.astype(jnp.bfloat16)

        def start_result(rank, carry):
            @pl.when(rank != me)
            def _():
                send_result(h, rank).start()

            @pl.when(rank == me)
            def _():
                pltpu.make_async_copy(
                    results.at[h, block_rows(me), :],
                    out_ref.at[0, :, columns(me, h)],
                    result_recv.at[h, me],
                ).start()

            return carry

        lax.fori_loop(0, ranks, start_result, 0)

    def compute_head(h, waits):
        wait_queries(h)
        start_state()

        def step(j, carry):
            if waits:
                pass_far(h, j + 1)
            middle_block(h, j)
            return carry

        lax.fori_loop(0, span, step, 0)
        last_block(h)

    read_lengths.wait()

    @pl.when(early)
    def _():
        for h in range(heads):
            pass_near(h)
        send_rest(orders[0][1])
        for h in range(heads):

            def step(i, carry, h=h):
                pass_far(h, span - i)
                return carry

            lax.fori_loop(0, span + 1, step, 0)
        for h in range(heads):
            compute_head(h, False)
        drain_rest(orders[0][1])

    @pl.when(late)
    def _():
        send_rest(orders[1][1])
        for h in range(heads):
            pass_near(h)
            pass_far(h, 0)
            compute_head(h, True)
        drain_rest(orders[1][1])

    for h in range(heads):

        def finish(i, carry, h=h):
            rank = lax.rem(me + i, ranks)
            send_result(h, rank).wait_send()
            return carry

        lax.fori_loop(1, ranks, finish, 0)

        @pl.when(span < spans - 1)
        def _(h=h):
            def finish_rank(rank, carry):
                def finish_span(j, carry):
                    forward(h, rank, j).wait_send()
                    return carry

                return lax.fori_loop(0, span + 1, finish_span, carry)

            lax.fori_loop(0, ranks, finish_rank, 0)

        def arrived(rank, carry, h=h):
            wait_bytes(out_ref.at[0, :, columns(rank, h)], result_recv.at[h, rank])
            return carry

        lax.fori_loop(0, ranks, arrived, 0)


def shards(spans, ranks, qkv, lengths):
    rows, features = qkv.shape[2], qkv.shape[3]
    heads = features // HD // ranks
    tokens = rows * ranks
    dma = pltpu.SemaphoreType.DMA
    return pl.pallas_call(
        functools.partial(kernel, spans, ranks, heads, rows),
        out_shape=jax.ShapeDtypeStruct((1, rows, features), jnp.bfloat16),
        in_specs=[
            pl.BlockSpec(memory_space=pltpu.HBM),
            pl.BlockSpec(memory_space=pltpu.HBM),
        ],
        out_specs=pl.BlockSpec(memory_space=pl.ANY),
        scratch_shapes=[
            pltpu.VMEM((heads, 2, spans, tokens, HD), jnp.bfloat16),
            pltpu.VMEM((heads, tokens, HD), jnp.bfloat16),
            pltpu.VMEM((heads, tokens, HD), jnp.bfloat16),
            pltpu.VMEM((1, tokens), jnp.float32),
            pltpu.VMEM((HD + 16, tokens), jnp.float32),
            pltpu.SMEM((spans,), jnp.int32),
            dma(()),
            dma((heads, ranks)),
            dma((heads, ranks)),
            dma((heads, ranks)),
            dma((heads, ranks, spans)),
            dma((heads, ranks, spans)),
            dma((heads, ranks)),
            dma((heads, ranks)),
        ],
        compiler_params=pltpu.CompilerParams(
            collective_id=0, has_side_effects=True, vmem_limit_bytes=64 * 2**20
        ),
    )(lengths, qkv)


def solution(mesh):
    in_specs = (P(None, "span", "seq", None), P())
    out_specs = P("span", "seq", None)
    body = functools.partial(shards, mesh.shape["span"], mesh.shape["seq"])
    return jax.shard_map(body, mesh=mesh, in_specs=in_specs, out_specs=out_specs, check_vma=False)
```

```python
import functools

import jax
import jax.numpy as jnp
from jax import lax
from jax.experimental import pallas as pl
from jax.experimental.pallas import tpu as pltpu
from jax.sharding import PartitionSpec as P

HD = 128
MASKED = -1e30
LOG2E = 1.4426950408889634
MESH = pl.DeviceIdType.MESH


def kernel(
    spans, ranks, heads, rows, lengths_hbm, qkv_ref, out_ref,
    keys, queries, results, peaks, sums, lengths_ref, lengths_sem,
    pair_send, query_send, result_send, forward_send,
    pair_recv, query_recv, result_recv,
):
    span = lax.axis_index("span")
    me = lax.axis_index("seq")
    tokens = rows * ranks
    query_tile = min(256, tokens)
    half = ranks // 2

    barrier = pltpu.get_barrier_semaphore()

    def greet(k, carry):
        pl.semaphore_signal(
            barrier, inc=1, device_id=(span, lax.rem(me + k, ranks)), device_id_type=MESH
        )
        return carry

    lax.fori_loop(1, ranks, greet, 0)

    @pl.when(span > 0)
    def _():
        pl.semaphore_signal(barrier, inc=1, device_id=(span - 1, me), device_id_type=MESH)

    @pl.when(span < spans - 1)
    def _():
        pl.semaphore_signal(barrier, inc=1, device_id=(span + 1, me), device_id_type=MESH)

    def block_rows(rank):
        return pl.ds(pl.multiple_of(rank * rows, rows), rows)

    def columns(rank, h):
        return pl.ds(pl.multiple_of((rank * heads + h) * HD, HD), HD)

    def pair_slot(h, rank, j):
        return keys.at[h, :, j, block_rows(rank), :]

    def query_slot(h, rank):
        return queries.at[h, block_rows(rank), :]

    def partner(k):
        total = 0
        for bit in range(ranks.bit_length() - 1):
            unit = 2**bit
            total += lax.rem(me // unit + k // unit, 2) * unit
        return total

    def send_step(i):
        odd = lax.rem(i, 2)
        return odd * ((i + 1) // 2) + (1 - odd) * (half + i // 2)

    def pair_source(rank, h):
        return qkv_ref.at[pl.ds(1, 2), 0, :, columns(rank, h)]

    def query_source(rank, h):
        return qkv_ref.at[0, 0, :, columns(rank, h)]

    def own_pair(h):
        return pltpu.make_async_copy(
            pair_source(me, h), pair_slot(h, me, span), pair_recv.at[h, me, span]
        )

    def own_query(h):
        return pltpu.make_async_copy(
            query_source(me, h), query_slot(h, me), query_recv.at[h, me]
        )

    def send_pair(h, rank):
        return pltpu.make_async_remote_copy(
            src_ref=pair_source(rank, h),
            dst_ref=pair_slot(h, me, span),
            send_sem=pair_send.at[h, rank],
            recv_sem=pair_recv.at[h, me, span],
            device_id=(span, rank),
            device_id_type=MESH,
        )

    def send_query(h, rank):
        return pltpu.make_async_remote_copy(
            src_ref=query_source(rank, h),
            dst_ref=query_slot(h, me),
            send_sem=query_send.at[h, rank],
            recv_sem=query_recv.at[h, me],
            device_id=(span, rank),
            device_id_type=MESH,
        )

    def send_result(h, rank):
        return pltpu.make_async_remote_copy(
            src_ref=results.at[h, block_rows(rank), :],
            dst_ref=out_ref.at[0, :, columns(me, h)],
            send_sem=result_send.at[h, rank],
            recv_sem=result_recv.at[h, me],
            device_id=(span, rank),
            device_id_type=MESH,
        )

    def forward(h, rank, j):
        return pltpu.make_async_remote_copy(
            src_ref=pair_slot(h, rank, j),
            dst_ref=pair_slot(h, rank, j),
            send_sem=forward_send.at[h, rank, j],
            recv_sem=pair_recv.at[h, rank, j],
            device_id=(span + 1, me),
            device_id_type=MESH,
        )

    def wait_bytes(ref, sem):
        pltpu.make_async_copy(ref, ref, sem).wait()

    read_lengths = pltpu.make_async_copy(lengths_hbm, lengths_ref, lengths_sem)
    read_lengths.start()
    for h in range(heads):
        own_pair(h).start()
        own_query(h).start()

    pl.semaphore_wait(
        barrier,
        ranks - 1 + (span > 0).astype(jnp.int32) + (span < spans - 1).astype(jnp.int32),
    )

    def start_group(h, make):
        def step(i, carry):
            make(h, partner(send_step(i))).start()
            return carry

        lax.fori_loop(0, ranks - 1, step, 0)

    def drain_group(h, make):
        def step(i, carry):
            make(h, partner(send_step(i))).wait_send()
            return carry

        lax.fori_loop(0, ranks - 1, step, 0)

    early = span < (spans + 1) // 2
    late = jnp.logical_not(early)
    last = span == spans - 1
    orders = (
        (early, [(h, make) for make in (send_pair, send_query) for h in range(heads)]),
        (late, [(h, make) for h in range(heads) for make in (send_query, send_pair)]),
    )
    ahead = min(3, 2 * heads)
    for here, order in orders:

        @pl.when(here)
        def _(order=order):
            for group in order[:ahead]:
                start_group(*group)

    def send_rest(order):
        for i in range(ahead, 2 * heads):
            drain_group(*order[i - ahead])
            start_group(*order[i])

    def drain_rest(order):
        for group in order[max(0, 2 * heads - ahead) :]:
            drain_group(*group)

    def pass_on(h, j, first, last):
        def step(k, carry):
            rank = partner(k)
            wait_bytes(pair_slot(h, rank, j), pair_recv.at[h, rank, j])

            @pl.when(span < spans - 1)
            def _():
                forward(h, rank, j).start()

            return carry

        lax.fori_loop(first, last, step, 0)

    def pass_near(h):
        def step(i, carry):
            pass_on(h, span - i, 0, half)
            return carry

        lax.fori_loop(0, span + 1, step, 0)

    def pass_far(h, j):
        pass_on(h, j, half, ranks)

    def wait_queries(h):
        def step(rank, carry):
            wait_bytes(query_slot(h, rank), query_recv.at[h, rank])
            return carry

        lax.fori_loop(0, ranks, step, 0)

    ones = jnp.ones((16, tokens), jnp.bfloat16)

    def add_block(h, j):
        k = keys[h, 0, j]
        v = jnp.concatenate([keys[h, 1, j].T, ones], axis=0)
        live = lax.broadcasted_iota(jnp.int32, (tokens, query_tile), 0) < lengths_ref[j]
        states = []
        for first in range(0, tokens, query_tile):
            here = pl.ds(first, query_tile)
            scores = lax.dot_general(
                k,
                queries[h, here, :],
                (((1,), (1,)), ((), ())),
                preferred_element_type=jnp.float32,
            )
            scores = jnp.where(live, scores, MASKED)
            peak = peaks[:, here]
            new_peak = jnp.maximum(peak, jnp.max(scores, axis=0, keepdims=True))
            weights = jnp.exp2((scores - new_peak) * (LOG2E * HD**-0.5)).astype(jnp.bfloat16)
            scale = jnp.exp2((peak - new_peak) * (LOG2E * HD**-0.5))
            acc = sums[:, here] * scale + jnp.dot(v, weights, preferred_element_type=jnp.float32)
            states.append((here, new_peak, acc))
        return states

    def start_state():
        peaks[...] = jnp.full(peaks.shape, MASKED, jnp.float32)
        sums[...] = jnp.zeros(sums.shape, jnp.float32)

    def middle_block(h, j):
        for here, peak, acc in add_block(h, j):
            peaks[:, here] = peak
            sums[:, here] = acc

    def last_block(h):
        for here, _, acc in add_block(h, span):
            position = here.start + lax.broadcasted_iota(jnp.int32, (HD, query_tile), 1)
            value = jnp.where(position < lengths_ref[span], acc[:HD] / acc[HD : HD + 1], 0.0)
            results[h, here, :] = value.T.astype(jnp.bfloat16)

        def start_result(rank, carry):
            @pl.when(rank != me)
            def _():
                send_result(h, rank).start()

            @pl.when(rank == me)
            def _():
                pltpu.make_async_copy(
                    results.at[h, block_rows(me), :],
                    out_ref.at[0, :, columns(me, h)],
                    result_recv.at[h, me],
                ).start()

            return carry

        lax.fori_loop(0, ranks, start_result, 0)

    def compute_head(h, waits):
        wait_queries(h)
        start_state()

        def step(j, carry):
            if waits:

                @pl.when(last)
                def _():
                    pass_far(h, j + 1)

            middle_block(h, j)
            return carry

        lax.fori_loop(0, span, step, 0)
        last_block(h)

    read_lengths.wait()

    @pl.when(early)
    def _():
        for h in range(heads):
            pass_near(h)
        send_rest(orders[0][1])
        for h in range(heads):

            def step(i, carry, h=h):
                pass_far(h, span - i)
                return carry

            lax.fori_loop(0, span + 1, step, 0)
        for h in range(heads):
            compute_head(h, False)
        drain_rest(orders[0][1])

    @pl.when(late)
    def _():
        send_rest(orders[1][1])

        @pl.when(jnp.logical_not(last))
        def _():
            for h in range(heads):
                pass_near(h)

                def step(j, carry, h=h):
                    pass_far(h, j)
                    return carry

                lax.fori_loop(0, span + 1, step, 0)

        for h in range(heads):

            @pl.when(last)
            def _(h=h):
                pass_near(h)
                pass_far(h, 0)

            compute_head(h, True)
        drain_rest(orders[1][1])

    for h in range(heads):

        def finish(i, carry, h=h):
            rank = lax.rem(me + i, ranks)
            send_result(h, rank).wait_send()
            return carry

        lax.fori_loop(1, ranks, finish, 0)

        @pl.when(span < spans - 1)
        def _(h=h):
            def finish_rank(rank, carry):
                def finish_span(j, carry):
                    forward(h, rank, j).wait_send()
                    return carry

                return lax.fori_loop(0, span + 1, finish_span, carry)

            lax.fori_loop(0, ranks, finish_rank, 0)

        def arrived(rank, carry, h=h):
            wait_bytes(out_ref.at[0, :, columns(rank, h)], result_recv.at[h, rank])
            return carry

        lax.fori_loop(0, ranks, arrived, 0)


def shards(spans, ranks, qkv, lengths):
    rows, features = qkv.shape[2], qkv.shape[3]
    heads = features // HD // ranks
    tokens = rows * ranks
    dma = pltpu.SemaphoreType.DMA
    return pl.pallas_call(
        functools.partial(kernel, spans, ranks, heads, rows),
        out_shape=jax.ShapeDtypeStruct((1, rows, features), jnp.bfloat16),
        in_specs=[
            pl.BlockSpec(memory_space=pltpu.HBM),
            pl.BlockSpec(memory_space=pltpu.HBM),
        ],
        out_specs=pl.BlockSpec(memory_space=pl.ANY),
        scratch_shapes=[
            pltpu.VMEM((heads, 2, spans, tokens, HD), jnp.bfloat16),
            pltpu.VMEM((heads, tokens, HD), jnp.bfloat16),
            pltpu.VMEM((heads, tokens, HD), jnp.bfloat16),
            pltpu.VMEM((1, tokens), jnp.float32),
            pltpu.VMEM((HD + 16, tokens), jnp.float32),
            pltpu.SMEM((spans,), jnp.int32),
            dma(()),
            dma((heads, ranks)),
            dma((heads, ranks)),
            dma((heads, ranks)),
            dma((heads, ranks, spans)),
            dma((heads, ranks, spans)),
            dma((heads, ranks)),
            dma((heads, ranks)),
        ],
        compiler_params=pltpu.CompilerParams(
            collective_id=0, has_side_effects=True, vmem_limit_bytes=64 * 2**20
        ),
    )(lengths, qkv)


def solution(mesh):
    in_specs = (P(None, "span", "seq", None), P())
    out_specs = P("span", "seq", None)
    body = functools.partial(shards, mesh.shape["span"], mesh.shape["seq"])
    return jax.shard_map(body, mesh=mesh, in_specs=in_specs, out_specs=out_specs, check_vma=False)
```

```python
import functools

import jax
import jax.numpy as jnp
from jax import lax
from jax.experimental import pallas as pl
from jax.experimental.pallas import tpu as pltpu
from jax.sharding import PartitionSpec as P

HD = 128
MASKED = -1e30
LOG2E = 1.4426950408889634
MESH = pl.DeviceIdType.MESH


def kernel(
    spans, ranks, heads, rows, lengths_hbm, qkv_ref, out_ref,
    keys, queries, results, peaks, sums, lengths_ref, lengths_sem,
    pair_send, query_send, result_send, forward_send,
    pair_recv, query_recv, result_recv,
):
    span = lax.axis_index("span")
    me = lax.axis_index("seq")
    tokens = rows * ranks
    query_tile = min(256, tokens)
    half = ranks // 2

    barrier = pltpu.get_barrier_semaphore()

    def greet(k, carry):
        pl.semaphore_signal(
            barrier, inc=1, device_id=(span, lax.rem(me + k, ranks)), device_id_type=MESH
        )
        return carry

    lax.fori_loop(1, ranks, greet, 0)

    @pl.when(span > 0)
    def _():
        pl.semaphore_signal(barrier, inc=1, device_id=(span - 1, me), device_id_type=MESH)

    @pl.when(span < spans - 1)
    def _():
        pl.semaphore_signal(barrier, inc=1, device_id=(span + 1, me), device_id_type=MESH)

    def block_rows(rank):
        return pl.ds(pl.multiple_of(rank * rows, rows), rows)

    def columns(rank, h):
        return pl.ds(pl.multiple_of((rank * heads + h) * HD, HD), HD)

    def pair_slot(h, rank, j):
        return keys.at[h, :, j, block_rows(rank), :]

    def query_slot(h, rank):
        return queries.at[h, block_rows(rank), :]

    def partner(k):
        total = 0
        for bit in range(ranks.bit_length() - 1):
            unit = 2**bit
            total += lax.rem(me // unit + k // unit, 2) * unit
        return total

    def send_step(i):
        odd = lax.rem(i, 2)
        return odd * ((i + 1) // 2) + (1 - odd) * (half + i // 2)

    def pair_source(rank, h):
        return qkv_ref.at[pl.ds(1, 2), 0, :, columns(rank, h)]

    def query_source(rank, h):
        return qkv_ref.at[0, 0, :, columns(rank, h)]

    def own_pair(h):
        return pltpu.make_async_copy(
            pair_source(me, h), pair_slot(h, me, span), pair_recv.at[h, me, span]
        )

    def own_query(h):
        return pltpu.make_async_copy(
            query_source(me, h), query_slot(h, me), query_recv.at[h, me]
        )

    def send_pair(h, rank):
        return pltpu.make_async_remote_copy(
            src_ref=pair_source(rank, h),
            dst_ref=pair_slot(h, me, span),
            send_sem=pair_send.at[h, rank],
            recv_sem=pair_recv.at[h, me, span],
            device_id=(span, rank),
            device_id_type=MESH,
        )

    def send_query(h, rank):
        return pltpu.make_async_remote_copy(
            src_ref=query_source(rank, h),
            dst_ref=query_slot(h, me),
            send_sem=query_send.at[h, rank],
            recv_sem=query_recv.at[h, me],
            device_id=(span, rank),
            device_id_type=MESH,
        )

    def send_result(h, rank):
        return pltpu.make_async_remote_copy(
            src_ref=results.at[h, block_rows(rank), :],
            dst_ref=out_ref.at[0, :, columns(me, h)],
            send_sem=result_send.at[h, rank],
            recv_sem=result_recv.at[h, me],
            device_id=(span, rank),
            device_id_type=MESH,
        )

    def forward(h, rank, j):
        return pltpu.make_async_remote_copy(
            src_ref=pair_slot(h, rank, j),
            dst_ref=pair_slot(h, rank, j),
            send_sem=forward_send.at[h, rank, j],
            recv_sem=pair_recv.at[h, rank, j],
            device_id=(span + 1, me),
            device_id_type=MESH,
        )

    def wait_bytes(ref, sem):
        pltpu.make_async_copy(ref, ref, sem).wait()

    read_lengths = pltpu.make_async_copy(lengths_hbm, lengths_ref, lengths_sem)
    read_lengths.start()
    for h in range(heads):
        own_pair(h).start()
        own_query(h).start()

    pl.semaphore_wait(
        barrier,
        ranks - 1 + (span > 0).astype(jnp.int32) + (span < spans - 1).astype(jnp.int32),
    )

    groups = [(h, make) for h in range(heads) for make in (send_pair, send_query)]
    in_flight = []

    def start_group(h, make):
        def step(i, carry):
            make(h, partner(send_step(i))).start()
            return carry

        lax.fori_loop(0, ranks - 1, step, 0)

    def drain_group(h, make):
        def step(i, carry):
            make(h, partner(send_step(i))).wait_send()
            return carry

        lax.fori_loop(0, ranks - 1, step, 0)

    def advance():
        if groups:
            if len(in_flight) == 2:
                drain_group(*in_flight.pop(0))
            in_flight.append(groups.pop(0))
            start_group(*in_flight[-1])

    advance()
    advance()

    def pass_on(h, j, first, last):
        def step(k, carry):
            rank = partner(k)
            wait_bytes(pair_slot(h, rank, j), pair_recv.at[h, rank, j])

            @pl.when(span < spans - 1)
            def _():
                forward(h, rank, j).start()

            return carry

        lax.fori_loop(first, last, step, 0)

    def pass_near(h):
        def step(i, carry):
            pass_on(h, span - i, 0, half)
            return carry

        lax.fori_loop(0, span + 1, step, 0)
        advance()

    def pass_far(h, j):
        pass_on(h, j, half, ranks)

    def wait_queries(h):
        def step(rank, carry):
            wait_bytes(query_slot(h, rank), query_recv.at[h, rank])
            return carry

        lax.fori_loop(0, ranks, step, 0)

    ones = jnp.ones((16, tokens), jnp.bfloat16)

    def add_block(h, j):
        k = keys[h, 0, j]
        v = jnp.concatenate([keys[h, 1, j].T, ones], axis=0)
        live = lax.broadcasted_iota(jnp.int32, (tokens, query_tile), 0) < lengths_ref[j]
        states = []
        for first in range(0, tokens, query_tile):
            here = pl.ds(first, query_tile)
            scores = lax.dot_general(
                k,
                queries[h, here, :],
                (((1,), (1,)), ((), ())),
                preferred_element_type=jnp.float32,
            )
            scores = jnp.where(live, scores, MASKED)
            peak = peaks[:, here]
            new_peak = jnp.maximum(peak, jnp.max(scores, axis=0, keepdims=True))
            weights = jnp.exp2((scores - new_peak) * (LOG2E * HD**-0.5)).astype(jnp.bfloat16)
            scale = jnp.exp2((peak - new_peak) * (LOG2E * HD**-0.5))
            acc = sums[:, here] * scale + jnp.dot(v, weights, preferred_element_type=jnp.float32)
            states.append((here, new_peak, acc))
        return states

    def start_state():
        peaks[...] = jnp.full(peaks.shape, MASKED, jnp.float32)
        sums[...] = jnp.zeros(sums.shape, jnp.float32)

    def middle_block(h, j):
        for here, peak, acc in add_block(h, j):
            peaks[:, here] = peak
            sums[:, here] = acc

    def last_block(h):
        for here, _, acc in add_block(h, 0):
            position = here.start + lax.broadcasted_iota(jnp.int32, (HD, query_tile), 1)
            value = jnp.where(position < lengths_ref[span], acc[:HD] / acc[HD : HD + 1], 0.0)
            results[h, here, :] = value.T.astype(jnp.bfloat16)

        def start_result(rank, carry):
            @pl.when(rank != me)
            def _():
                send_result(h, rank).start()

            @pl.when(rank == me)
            def _():
                pltpu.make_async_copy(
                    results.at[h, block_rows(me), :],
                    out_ref.at[0, :, columns(me, h)],
                    result_recv.at[h, me],
                ).start()

            return carry

        lax.fori_loop(0, ranks, start_result, 0)

    read_lengths.wait()
    pass_near(0)
    for h in range(heads):
        start_state()
        pass_far(h, span)

        @pl.when(span > 0)
        def _(h=h):
            pass_far(h, span - 1)

        advance()
        wait_queries(h)

        def step(i, carry, h=h):
            middle_block(h, span - i)

            @pl.when(i + 1 < span)
            def _():
                pass_far(h, span - i - 2)

            return carry

        lax.fori_loop(0, span, step, 0)
        if h + 1 < heads:
            pass_near(h + 1)
        last_block(h)

    for group in in_flight:
        drain_group(*group)

    for h in range(heads):

        def finish(i, carry, h=h):
            rank = lax.rem(me + i, ranks)
            send_result(h, rank).wait_send()
            return carry

        lax.fori_loop(1, ranks, finish, 0)

        @pl.when(span < spans - 1)
        def _(h=h):
            def finish_rank(rank, carry):
                def finish_span(j, carry):
                    forward(h, rank, j).wait_send()
                    return carry

                return lax.fori_loop(0, span + 1, finish_span, carry)

            lax.fori_loop(0, ranks, finish_rank, 0)

        def arrived(rank, carry, h=h):
            wait_bytes(out_ref.at[0, :, columns(rank, h)], result_recv.at[h, rank])
            return carry

        lax.fori_loop(0, ranks, arrived, 0)


def shards(spans, ranks, qkv, lengths):
    rows, features = qkv.shape[2], qkv.shape[3]
    heads = features // HD // ranks
    tokens = rows * ranks
    dma = pltpu.SemaphoreType.DMA
    return pl.pallas_call(
        functools.partial(kernel, spans, ranks, heads, rows),
        out_shape=jax.ShapeDtypeStruct((1, rows, features), jnp.bfloat16),
        in_specs=[
            pl.BlockSpec(memory_space=pltpu.HBM),
            pl.BlockSpec(memory_space=pltpu.HBM),
        ],
        out_specs=pl.BlockSpec(memory_space=pl.ANY),
        scratch_shapes=[
            pltpu.VMEM((heads, 2, spans, tokens, HD), jnp.bfloat16),
            pltpu.VMEM((heads, tokens, HD), jnp.bfloat16),
            pltpu.VMEM((heads, tokens, HD), jnp.bfloat16),
            pltpu.VMEM((1, tokens), jnp.float32),
            pltpu.VMEM((HD + 16, tokens), jnp.float32),
            pltpu.SMEM((spans,), jnp.int32),
            dma(()),
            dma((heads, ranks)),
            dma((heads, ranks)),
            dma((heads, ranks)),
            dma((heads, ranks, spans)),
            dma((heads, ranks, spans)),
            dma((heads, ranks)),
            dma((heads, ranks)),
        ],
        compiler_params=pltpu.CompilerParams(
            collective_id=0, has_side_effects=True, vmem_limit_bytes=64 * 2**20
        ),
    )(lengths, qkv)


def solution(mesh):
    in_specs = (P(None, "span", "seq", None), P())
    out_specs = P("span", "seq", None)
    body = functools.partial(shards, mesh.shape["span"], mesh.shape["seq"])
    return jax.shard_map(body, mesh=mesh, in_specs=in_specs, out_specs=out_specs, check_vma=False)
```
